32 devices in a mesh: dp: 8 (over z, y), ctx: 4 (over x, core).
Axes of the slice: x: 2, y: 2, z: 4, core: 2. Of those that a mesh axis runs over, the one named last changes fastest.
Arguments:
- projected: bfloat16 [2, 8, 512, 4096], P(None, 'dp', 'ctx'), may hold values from -6 to 6
- token_ids: int32 [8, 512], P('dp', 'ctx'), may hold values from 0 to 511
- short_filters: float32 [2, 7, 4096], P(None, None, 'ctx'), may hold values from -2 to 2
- medium_filter: bfloat16 [128, 4096], P(None, 'ctx'), may hold values from -0.75 to 0.75
- skip_gain: float32 [4096], P('ctx'), may hold values from -3 to 3
Outputs:
- grad_projected: bfloat16 [2, 8, 512, 4096], P(None, 'dp', 'ctx')
- grad_short: float32 [2, 7, 4096], P(None, None, 'ctx')
- grad_medium: float32 [128, 4096], P(None, 'ctx')
- grad_skip: float32 [4096], P('ctx')
The draws below stay inside these ranges and needn't reach their ends.
All inputs are finite; a program needn't handle non-finite values.
Results may differ from the reference program's by a relative error of at most 0.024.
Values may be sent and summed in bfloat16 or wider, within the bound.
A program may use at most 128 MiB of HBM per device.

```python
import jax
import jax.numpy as jnp
from jax import lax

C = 4096
FILT = 128
SHORT = 7
SEQS = 8
LEN = 512


def with_ends(array, own_key, least, top_value):
    place = [jax.random.randint(jax.random.fold_in(own_key, axis), (), 0, length) for axis, length in enumerate(array.shape)]
    main_axis = array.shape.index(max(array.shape))
    beside = place[:main_axis] + [(place[main_axis] + 1) % array.shape[main_axis]] + place[main_axis + 1:]
    return array.at[tuple(place)].set(least).at[tuple(beside)].set(top_value)


def block_levels(own_key, extent, shards, smallest, largest):
    level = 1.0
    for axis_at, parts in shards:
        draws = jax.random.uniform(jax.random.fold_in(jax.random.fold_in(own_key, 6), axis_at), (parts,), jnp.float32, smallest / len(shards), largest / len(shards))
        level = level * jnp.repeat(jnp.exp(draws), extent[axis_at] // parts).reshape((-1,) + (1,) * (len(extent) - 1 - axis_at))
    return level


def scatter_about(rng, dims, deviation, most, cuts=(), dtype=jnp.bfloat16):
    loudness = block_levels(rng, dims, cuts, -0.22, 0.18) if cuts else 1.0
    array = jax.random.normal(rng, dims, jnp.float32) * deviation * loudness
    return jnp.minimum(jnp.maximum(array, -most), most).astype(dtype)


def setup_inputs(seed: int = 0) -> dict:
    streams_of = jax.random.split(jax.random.key(seed), 6)
    projected = scatter_about(streams_of[0], (2, SEQS, LEN, C), 1.0, 6.0, ((1, 8), (2, 4)))
    token_ids = with_ends(jax.random.randint(streams_of[1], (SEQS, LEN), 0, 512), jax.random.fold_in(streams_of[1], 1), 0, 511).astype(jnp.int32)
    short_filters = scatter_about(streams_of[2], (2, SHORT, C), SHORT ** -0.5, 2.0, ((2, 4),), jnp.float32)
    medium_filter = scatter_about(streams_of[3], (FILT, C), (FILT // 2) ** -0.5, 0.75, ((1, 4),))
    skip_gain = scatter_about(streams_of[4], (C,), 0.5, 3.0, ((0, 4),), jnp.float32)
    return dict(projected=projected, token_ids=token_ids, short_filters=short_filters, medium_filter=medium_filter, skip_gain=skip_gain)


def short_forward(extended, filters):
    short_len = filters.shape[1]
    length = extended.shape[1] - short_len + 1
    result = jnp.zeros((extended.shape[0], length, extended.shape[2]), jnp.float32)
    for offset in range(short_len):
        start = short_len - 1 - offset
        result = result + filters[:, offset][:, None, :] * extended[:, start:start + length].astype(jnp.float32)
    return result


def short_backward(extended, filters):
    short_len = filters.shape[1]
    length = extended.shape[1] - short_len + 1
    result = jnp.zeros((extended.shape[0], length, extended.shape[2]), jnp.float32)
    for offset in range(short_len):
        result = result + filters[:, offset][:, None, :] * extended[:, offset:offset + length].astype(jnp.float32)
    return result


def short_weights(grads, extended):
    short_len = extended.shape[1] - grads.shape[1] + 1
    length = grads.shape[1]
    rows = []
    for offset in range(short_len):
        start = short_len - 1 - offset
        rows.append(jnp.sum(grads.astype(jnp.float32) * extended[:, start:start + length].astype(jnp.float32), axis=1))
    return jnp.stack(rows, axis=1)


def causal_fft(signal, kernel):
    length = signal.shape[0]
    total = length + kernel.shape[0]
    spectrum = jnp.fft.rfft(signal, n=total, axis=0) * jnp.fft.rfft(kernel, n=total, axis=0)
    return jnp.fft.irfft(spectrum, n=total, axis=0)[:length]


def anti_fft(signal, kernel):
    length = signal.shape[0]
    total = length + kernel.shape[0]
    spectrum = jnp.conj(jnp.fft.rfft(kernel, n=total, axis=0)) * jnp.fft.rfft(signal, n=total, axis=0)
    return jnp.fft.irfft(spectrum, n=total, axis=0)[:length]


def lag_fft(later, earlier, taps):
    total = later.shape[0] + taps
    spectrum = jnp.conj(jnp.fft.rfft(earlier, n=total, axis=0)) * jnp.fft.rfft(later, n=total, axis=0)
    return jnp.fft.irfft(spectrum, n=total, axis=0)[:taps]


def reference(projected, token_ids, short_filters, medium_filter, skip_gain):
    short_len = short_filters.shape[1]
    filter_len = medium_filter.shape[0]
    medium = medium_filter.astype(jnp.float32)

    def one_sequence(items):
        inputs, idents = items
        loss_weight = jnp.where((idents >= 97) & (idents <= 122), 0.1, 1.0).astype(jnp.bfloat16)
        padded_inputs = jnp.pad(inputs, ((0, 0), (short_len - 1, 0), (0, 0)))
        filtered = short_forward(padded_inputs, short_filters)
        product = (filtered[0] * filtered[1]).astype(jnp.bfloat16)
        product_f = product.astype(jnp.float32)
        mix = causal_fft(product_f, medium) + skip_gain * product_f
        grad_mix = (loss_weight.astype(jnp.float32)[:, None] * mix).astype(jnp.bfloat16)
        grad_mix_f = grad_mix.astype(jnp.float32)
        back_product = anti_fft(grad_mix_f, medium) + skip_gain * grad_mix_f
        grad_key = (back_product * filtered[1]).astype(jnp.bfloat16)
        grad_value = (back_product * filtered[0]).astype(jnp.bfloat16)
        grad_filtered = jnp.stack([grad_key, grad_value])
        padded_grads = jnp.pad(grad_filtered, ((0, 0), (0, short_len - 1), (0, 0)))
        grad_inputs = short_backward(padded_grads, short_filters).astype(jnp.bfloat16)
        grad_taps = lag_fft(grad_mix_f, product_f, filter_len)
        grad_gain = jnp.sum(grad_mix_f * product_f, axis=0)
        grad_short = short_weights(grad_filtered, padded_inputs)
        return grad_inputs, grad_short, grad_taps, grad_gain

    results = lax.map(one_sequence, (jnp.moveaxis(projected, 1, 0), token_ids))
    grad_projected = jnp.moveaxis(results[0], 0, 1)
    grad_short = jnp.sum(results[1], axis=0) / SEQS
    grad_medium = jnp.sum(results[2], axis=0) / SEQS
    grad_skip = jnp.sum(results[3], axis=0) / SEQS
    return grad_projected, grad_short, grad_medium, grad_skip
```

```python
import functools

import jax
import jax.numpy as jnp
import ml_dtypes
import numpy as np
from jax import lax
from jax.experimental import pallas as pl
from jax.experimental.pallas import tpu as pltpu
from jax.sharding import PartitionSpec as P

MESH = pl.DeviceIdType.MESH
F32 = jnp.float32
BF16 = jnp.bfloat16
LANES = 128
EDGE = 16


def transform_table(block):
    bins = np.concatenate([np.arange(0, block, 2), np.arange(1, block, 2)])
    angle = 2 * np.pi * np.outer(bins + 0.5, np.arange(block)) / (2 * block)
    return np.concatenate([np.cos(angle), -np.sin(angle)])


def quarter_turn(spec):
    half = spec.shape[0] // 4
    re_even, re_odd = spec[:half], spec[half : 2 * half]
    im_even, im_odd = spec[2 * half : 3 * half], spec[3 * half :]
    return jnp.concatenate([-im_even, im_odd, re_even, -re_odd], axis=0)


def times(a, b):
    half = a.shape[0] // 2
    ar, ai, br, bi = a[:half], a[half:], b[:half], b[half:]
    return jnp.concatenate([ar * br - ai * bi, ar * bi + ai * br], axis=0)


def times_conj(a, b):
    half = a.shape[0] // 2
    ar, ai, br, bi = a[:half], a[half:], b[:half], b[half:]
    return jnp.concatenate([ar * br + ai * bi, ai * br - ar * bi], axis=0)


def kernel(
    n,
    chunks,
    x_ref,
    tok_ref,
    short_ref,
    medium_ref,
    skip_ref,
    fwd_ref,
    inv_ref,
    out_ref,
    grads_ref,
    xin,
    xf,
    filt,
    sfull,
    wrow,
    wtile,
    prod_send,
    prod_recv,
    b_send,
    b_recv,
    out_v,
    gbuf,
    gs_f,
    gs_send,
    gs_recv,
    zs,
    gspec,
    gmix,
    halo_ssem,
    halo_rsem,
    small_ssem,
    small_rsem,
    p_ssem,
    p_rsem,
    b_ssem,
    b_rsem,
    g_ssem,
    g_rsem,
    in_sem,
    out_sem,
):
    me = lax.axis_index("ctx")
    dp = lax.axis_index("dp")
    block = x_ref.shape[1]
    own = medium_ref.shape[1]
    width = own // chunks
    tiles = width // LANES
    short_len = short_ref.shape[1]
    rows = block + EDGE
    order = [d for d in (2, 1, 3) if d < n] + [d for d in range(4, n)]

    def peer(d):
        return lax.rem(me + d, n)

    def remote(src, dst, ssem, rsem, to):
        return pltpu.make_async_remote_copy(
            src_ref=src,
            dst_ref=dst,
            send_sem=ssem,
            recv_sem=rsem,
            device_id=(dp, to),
            device_id_type=MESH,
        )

    local_in = pltpu.make_async_copy(x_ref, xin.at[:, pl.ds(EDGE, block), :], in_sem)
    local_in.start()
    tokens = tok_ref[...]
    weight = jnp.where((tokens >= 97) & (tokens <= 122), 0.1, 1.0).astype(BF16).astype(F32)
    wrow[me] = jnp.broadcast_to(weight, (8, block))
    sfull[me] = short_ref[...]

    barrier = pltpu.get_barrier_semaphore()
    for d in order:
        pl.semaphore_signal(barrier, inc=1, device_id=(dp, peer(d)), device_id_type=MESH)
    pl.semaphore_wait(barrier, n - 1)

    later = lax.rem(me + 1, n)
    earlier = lax.rem(me + n - 1, n)
    to_later = remote(
        x_ref.at[:, pl.ds(block - EDGE, EDGE), :],
        xin.at[:, pl.ds(0, EDGE), :],
        halo_ssem.at[0],
        halo_rsem.at[0],
        later,
    )
    to_earlier = remote(
        x_ref.at[:, pl.ds(0, EDGE), :],
        xin.at[:, pl.ds(block + EDGE, EDGE), :],
        halo_ssem.at[1],
        halo_rsem.at[1],
        earlier,
    )

    @pl.when(me < n - 1)
    def _():
        to_later.start()

    @pl.when(me > 0)
    def _():
        to_earlier.start()

    def small_copies(d, source):
        return (
            remote(
                sfull.at[source],
                sfull.at[source],
                small_ssem.at[0, d],
                small_rsem.at[0, source],
                peer(d),
            ),
            remote(
                wrow.at[source],
                wrow.at[source],
                small_ssem.at[1, d],
                small_rsem.at[1, source],
                peer(d),
            ),
        )

    for d in order:
        for copy in small_copies(d, me):
            copy.start()

    zero_edge = jnp.zeros((2, EDGE, xin.shape[2]), BF16)

    @pl.when(me == 0)
    def _():
        xin[:, pl.ds(0, EDGE), :] = zero_edge

    @pl.when(me == n - 1)
    def _():
        xin[:, pl.ds(block + EDGE, EDGE), :] = zero_edge

    b_send[pl.ds(n * block, EDGE), :] = jnp.zeros((EDGE, own), BF16)
    gs_f[...] = jnp.zeros_like(gs_f)

    for d in order:
        for copy in small_copies(d, peer(d)):
            copy.wait_recv()
    for o in range(n):
        wtile[pl.ds(o * block, block), :] = jnp.broadcast_to(wrow[o, 0:1, :], (LANES, block)).T
    local_in.wait()

    @pl.when(me > 0)
    def _():
        to_later.wait_recv()

    @pl.when(me < n - 1)
    def _():
        to_earlier.wait_recv()

    def columns(owner, k):
        return pl.ds(pl.multiple_of(owner * own + k * width, LANES), width)

    def prod_copy(k, d, source):
        return remote(
            prod_send.at[:, columns(peer(d), k)],
            prod_recv.at[pl.ds(pl.multiple_of(source * block, block), block), columns(0, k)],
            p_ssem.at[k, d],
            p_rsem.at[k, source],
            peer(d),
        )

    def back_copy(k, d, source):
        return remote(
            b_send.at[pl.ds(pl.multiple_of(peer(d) * block, block), rows), columns(0, k)],
            b_recv.at[:, columns(source, k)],
            b_ssem.at[k, d],
            b_rsem.at[k, source],
            peer(d),
        )

    def short_copy(k, d, source):
        return remote(
            gs_send.at[:, columns(peer(d), k)],
            gs_recv.at[source, :, columns(0, k)],
            g_ssem.at[k, d],
            g_rsem.at[k, source],
            peer(d),
        )

    def out_copy(k, owner):
        return pltpu.make_async_copy(
            out_v.at[:, :, columns(owner, k)],
            out_ref.at[:, :, columns(owner, k)],
            out_sem.at[k, owner],
        )

    def products(k):
        for d in order + [0]:
            owner = peer(d)

            @pl.loop(0, tiles)
            def _(tile):
                inner = pl.ds(pl.multiple_of(k * width + tile * LANES, LANES), LANES)
                cols = pl.ds(pl.multiple_of(owner * own + k * width + tile * LANES, LANES), LANES)
                for s in range(2):
                    xf[s, :, cols] = xin[s, :, cols].astype(F32)
                    total = jnp.zeros((rows, LANES), F32)
                    for i in range(short_len):
                        total += sfull[owner, s, i : i + 1, inner] * xf[s, pl.ds(EDGE - i, rows), cols]
                    filt[s, :, cols] = total
                product = (filt[0, pl.ds(0, block), cols] * filt[1, pl.ds(0, block), cols]).astype(BF16)
                if d == 0:
                    prod_recv[pl.ds(pl.multiple_of(me * block, block), block), inner] = product
                else:
                    prod_send[:, cols] = product

            if d != 0:
                prod_copy(k, d, me).start()

    def medium(k):
        for d in order:
            prod_copy(k, d, peer(d)).wait_recv()
        cols = columns(0, k)
        fwd = fwd_ref[...]
        inv = inv_ref[...]
        skip = skip_ref[:, cols]

        def block_rows(f):
            return pl.ds(f * block, block)

        def dot(a, b):
            return jnp.dot(a, b, preferred_element_type=F32)

        response = dot(fwd, medium_ref[:, cols])
        for f in range(n):
            gspec[f] = dot(fwd, prod_recv[block_rows(f), cols])
        for f in range(n):
            zs[f] = gspec[f] + quarter_turn(gspec[f - 1]) if f else gspec[f]
        gain = jnp.zeros((1, width), F32)
        for f in range(n):
            product = prod_recv[block_rows(f), cols].astype(F32)
            mix = dot(inv, times(response, zs[f]).astype(BF16)) + skip * product
            weights = jnp.concatenate([wtile[block_rows(f), :]] * tiles, axis=1)
            grad = (weights * mix).astype(BF16)
            gmix[block_rows(f), :] = grad
            gain += jnp.sum(grad.astype(F32) * product, axis=0, keepdims=True)
        for f in range(n):
            gspec[f] = dot(fwd, gmix[block_rows(f), :])
        cross = jnp.zeros((2 * block, width), F32)
        for f in range(n):
            cross += times_conj(gspec[f], zs[f])
        for f in range(n):
            spec = gspec[f] - quarter_turn(gspec[f + 1]) if f < n - 1 else gspec[f]
            back = dot(inv, times_conj(spec, response).astype(BF16))
            back += skip * gmix[block_rows(f), :].astype(F32)
            b_send[block_rows(f), cols] = back.astype(BF16)
        for d in order:
            back_copy(k, d, me).start()
        high = cross.astype(BF16)
        low = (cross - high.astype(F32)).astype(BF16)
        grads_ref[pl.ds(0, block), cols] = (dot(inv, high) + dot(inv, low)).astype(BF16)
        gs_f[2 * short_len : 2 * short_len + 1, columns(me, k)] = gain

    def shorts(k):
        for d in [0] + order:
            owner = peer(d)
            if d != 0:
                back_copy(k, d, owner).wait_recv()

            @pl.loop(0, tiles)
            def _(tile):
                inner = pl.ds(pl.multiple_of(k * width + tile * LANES, LANES), LANES)
                cols = pl.ds(pl.multiple_of(owner * own + k * width + tile * LANES, LANES), LANES)
                if d == 0:
                    back = b_send[pl.ds(pl.multiple_of(me * block, block), rows), inner].astype(F32)
                else:
                    back = b_recv[:, cols].astype(F32)
                for s in range(2):
                    gbuf[s] = (back * filt[1 - s, :, cols]).astype(BF16).astype(F32)
                    total = jnp.zeros((block, LANES), F32)
                    grad = gbuf[s, pl.ds(0, block), :]
                    for i in range(short_len):
                        total += sfull[owner, s, i : i + 1, inner] * gbuf[s, pl.ds(i, block), :]
                        row = s * short_len + i
                        gs_f[row : row + 1, cols] = jnp.sum(
                            grad * xf[s, pl.ds(EDGE - i, block), cols], axis=0, keepdims=True
                        )
                    out_v[s, :, cols] = total.astype(BF16)

            out_copy(k, owner).start()
            if d != 0:
                gs_send[:, columns(owner, k)] = gs_f[:, columns(owner, k)].astype(BF16)
                short_copy(k, d, me).start()

    @pl.loop(0, chunks + 2)
    def _(step):
        @pl.when(step < chunks)
        def _():
            products(step)

        @pl.when((step >= 1) & (step <= chunks))
        def _():
            medium(step - 1)

        @pl.when(step >= 2)
        def _():
            shorts(step - 2)

    @pl.loop(0, chunks)
    def _(k):
        total = gs_f[:, columns(me, k)]
        for d in order:
            short_copy(k, d, peer(d)).wait_recv()
            total += gs_recv[peer(d), :, columns(0, k)].astype(F32)
        grads_ref[pl.ds(block, EDGE), columns(0, k)] = total.astype(BF16)
        for d in order:
            prod_copy(k, d, me).wait_send()
            back_copy(k, d, me).wait_send()
            short_copy(k, d, me).wait_send()
        for o in range(n):
            out_copy(k, o).wait()

    for d in order:
        for copy in small_copies(d, me):
            copy.wait_send()

    @pl.when(me < n - 1)
    def _():
        to_later.wait_send()

    @pl.when(me > 0)
    def _():
        to_earlier.wait_send()


def local(projected, token_ids, short_filters, medium_filter, skip_gain):
    inputs = projected[:, 0]
    _, block, channels = inputs.shape
    short_len = short_filters.shape[1]
    own = medium_filter.shape[1]
    groups = lax.axis_size("dp")
    n = lax.axis_size("ctx")
    chunks = max(1, own // 256)
    width = own // chunks
    table = transform_table(block)
    forward = jnp.asarray(table.astype(ml_dtypes.bfloat16))
    inverse = jnp.asarray((table.T / block).astype(ml_dtypes.bfloat16))
    rows = block + EDGE
    vmem = pl.BlockSpec(memory_space=pltpu.VMEM)
    hbm = pl.BlockSpec(memory_space=pl.ANY)
    dma = pltpu.SemaphoreType.DMA
    out, grads = pl.pallas_call(
        functools.partial(kernel, n, chunks),
        out_shape=(
            jax.ShapeDtypeStruct(inputs.shape, BF16),
            jax.ShapeDtypeStruct((rows, own), BF16),
        ),
        in_specs=[hbm, vmem, vmem, vmem, vmem, vmem, vmem],
        out_specs=(hbm, vmem),
        scratch_shapes=[
            pltpu.VMEM((2, block + 2 * EDGE, channels), BF16),
            pltpu.VMEM((2, block + 2 * EDGE, channels), F32),
            pltpu.VMEM((2, rows, channels), F32),
            pltpu.VMEM((n, 2, short_len, own), F32),
            pltpu.VMEM((n, 8, block), F32),
            pltpu.VMEM((n * block, LANES), F32),
            pltpu.VMEM((block, channels), BF16),
            pltpu.VMEM((n * block, own), BF16),
            pltpu.VMEM((n * block + EDGE, own), BF16),
            pltpu.VMEM((rows, channels), BF16),
            pltpu.VMEM((2, block, channels), BF16),
            pltpu.VMEM((2, rows, LANES), F32),
            pltpu.VMEM((EDGE, channels), F32),
            pltpu.VMEM((EDGE, channels), BF16),
            pltpu.VMEM((n, EDGE, own), BF16),
            pltpu.VMEM((n, 2 * block, width), F32),
            pltpu.VMEM((n, 2 * block, width), F32),
            pltpu.VMEM((n * block, width), BF16),
            dma((2,)),
            dma((2,)),
            dma((2, n)),
            dma((2, n)),
            dma((chunks, n)),
            dma((chunks, n)),
            dma((chunks, n)),
            dma((chunks, n)),
            dma((chunks, n)),
            dma((chunks, n)),
            dma,
            dma((chunks, n)),
        ],
        compiler_params=pltpu.CompilerParams(
            collective_id=0, has_side_effects=True, vmem_limit_bytes=48 * 1024 * 1024
        ),
    )(inputs, token_ids, short_filters, medium_filter, skip_gain[None], forward, inverse)
    grads = lax.psum(grads, "dp").astype(F32) / groups
    taps = grads[:block]
    short = grads[block : block + 2 * short_len].reshape(2, short_len, own)
    gain = grads[block + 2 * short_len]
    return out[:, None], short, taps, gain


def solution(mesh):
    placed = (
        P(None, "dp", "ctx", None),
        P("dp", "ctx"),
        P(None, None, "ctx"),
        P(None, "ctx"),
        P("ctx"),
    )
    return jax.shard_map(
        local,
        mesh=mesh,
        in_specs=placed,
        out_specs=(P(None, "dp", "ctx", None), P(None, None, "ctx"), P(None, "ctx"), P("ctx")),
        check_vma=False,
    )
```

```python
import functools

import jax
import jax.numpy as jnp
import ml_dtypes
import numpy as np
from jax import lax
from jax.experimental import pallas as pl
from jax.experimental.pallas import tpu as pltpu
from jax.sharding import PartitionSpec as P

MESH = pl.DeviceIdType.MESH
F32 = jnp.float32
BF16 = jnp.bfloat16
LANES = 128
EDGE = 16


def transform_table(block):
    bins = np.concatenate([np.arange(0, block, 2), np.arange(1, block, 2)])
    angle = 2 * np.pi * np.outer(bins + 0.5, np.arange(block)) / (2 * block)
    return np.concatenate([np.cos(angle), -np.sin(angle)])


def quarter_turn(spec):
    half = spec.shape[0] // 4
    re_even, re_odd = spec[:half], spec[half : 2 * half]
    im_even, im_odd = spec[2 * half : 3 * half], spec[3 * half :]
    return jnp.concatenate([-im_even, im_odd, re_even, -re_odd], axis=0)


def times(a, b):
    half = a.shape[0] // 2
    ar, ai, br, bi = a[:half], a[half:], b[:half], b[half:]
    return jnp.concatenate([ar * br - ai * bi, ar * bi + ai * br], axis=0)


def times_conj(a, b):
    half = a.shape[0] // 2
    ar, ai, br, bi = a[:half], a[half:], b[:half], b[half:]
    return jnp.concatenate([ar * br + ai * bi, ai * br - ar * bi], axis=0)


def kernel(
    n,
    groups,
    chunks,
    fused,
    x_ref,
    tok_hbm,
    short_hbm,
    medium_hbm,
    skip_hbm,
    fwd_hbm,
    inv_hbm,
    out_ref,
    taps_ref,
    short_out,
    gain_ref,
    tok_ref,
    medium_ref,
    skip_ref,
    fwd_ref,
    inv_ref,
    part,
    part_recv,
    piece,
    gathered,
    gs_sum,
    gs_all,
    xin,
    xf,
    filt,
    sfull,
    wrow,
    wtile,
    prod_send,
    prod_recv,
    b_send,
    b_recv,
    out_v,
    gbuf,
    gs_f,
    gs_send,
    gs_recv,
    zs,
    gspec,
    gmix,
    halo_ssem,
    halo_rsem,
    small_ssem,
    small_rsem,
    p_ssem,
    p_rsem,
    b_ssem,
    b_rsem,
    g_ssem,
    g_rsem,
    r_ssem,
    r_rsem,
    a_ssem,
    a_rsem,
    t_ssem,
    t_rsem,
    in_sem,
    out_sem,
):
    me = lax.axis_index("ctx")
    dp = lax.axis_index("dp")
    block = x_ref.shape[1]
    own = medium_ref.shape[1]
    width = own // chunks
    tiles = width // LANES
    short_len = short_hbm.shape[0]
    rows = block + EDGE
    order = [d for d in (2, 1, 3) if d < n] + [d for d in range(4, n)]

    def peer(d):
        return lax.rem(me + d, n)

    def mate(e):
        return lax.rem(dp + e, groups)

    mates = range(1, groups) if fused else ()

    def remote(src, dst, ssem, rsem, to, group=None):
        return pltpu.make_async_remote_copy(
            src_ref=src,
            dst_ref=dst,
            send_sem=ssem,
            recv_sem=rsem,
            device_id=(dp if group is None else group, to),
            device_id_type=MESH,
        )

    loads = [
        pltpu.make_async_copy(src, dst, in_sem.at[j])
        for j, (src, dst) in enumerate(
            (
                (tok_hbm, tok_ref),
                (short_hbm, sfull.at[me]),
                (x_ref, xin.at[:, pl.ds(EDGE, block), :]),
                (medium_hbm, medium_ref),
                (skip_hbm, skip_ref),
                (fwd_hbm, fwd_ref),
                (inv_hbm, inv_ref),
            )
        )
    ]
    for load in loads:
        load.start()
    loads[0].wait()
    tokens = tok_ref[...]
    weight = jnp.where((tokens >= 97) & (tokens <= 122), 0.1, 1.0).astype(BF16).astype(F32)
    wrow[me] = jnp.broadcast_to(weight, (8, block))

    barrier = pltpu.get_barrier_semaphore()
    for d in order:
        pl.semaphore_signal(barrier, inc=1, device_id=(dp, peer(d)), device_id_type=MESH)
    for e in mates:
        pl.semaphore_signal(barrier, inc=1, device_id=(mate(e), me), device_id_type=MESH)
    pl.semaphore_wait(barrier, n - 1 + len(mates))

    later = lax.rem(me + 1, n)
    earlier = lax.rem(me + n - 1, n)
    to_later = remote(
        x_ref.at[:, pl.ds(block - EDGE, EDGE), :],
        xin.at[:, pl.ds(0, EDGE), :],
        halo_ssem.at[0],
        halo_rsem.at[0],
        later,
    )
    to_earlier = remote(
        x_ref.at[:, pl.ds(0, EDGE), :],
        xin.at[:, pl.ds(block + EDGE, EDGE), :],
        halo_ssem.at[1],
        halo_rsem.at[1],
        earlier,
    )

    @pl.when(me < n - 1)
    def _():
        to_later.start()

    @pl.when(me > 0)
    def _():
        to_earlier.start()

    def small_copies(d, source):
        return (
            remote(
                sfull.at[source],
                sfull.at[source],
                small_ssem.at[0, d],
                small_rsem.at[0, source],
                peer(d),
            ),
            remote(
                wrow.at[source],
                wrow.at[source],
                small_ssem.at[1, d],
                small_rsem.at[1, source],
                peer(d),
            ),
        )

    loads[1].wait()
    for d in order:
        for copy in small_copies(d, me):
            copy.start()

    zero_edge = jnp.zeros((2, EDGE, xin.shape[2]), BF16)

    @pl.when(me == 0)
    def _():
        xin[:, pl.ds(0, EDGE), :] = zero_edge

    @pl.when(me == n - 1)
    def _():
        xin[:, pl.ds(block + EDGE, EDGE), :] = zero_edge

    b_send[pl.ds(n * block, EDGE), :] = jnp.zeros((EDGE, own), BF16)
    gs_f[...] = jnp.zeros_like(gs_f)

    for d in order:
        for copy in small_copies(d, peer(d)):
            copy.wait_recv()
    for o in range(n):
        wtile[pl.ds(o * block, block), :] = jnp.broadcast_to(wrow[o, 0:1, :], (LANES, block)).T
    for load in loads[2:]:
        load.wait()

    @pl.when(me > 0)
    def _():
        to_later.wait_recv()

    @pl.when(me < n - 1)
    def _():
        to_earlier.wait_recv()

    def columns(owner, k):
        return pl.ds(pl.multiple_of(owner * own + k * width, LANES), width)

    def prod_copy(k, d, source):
        return remote(
            prod_send.at[:, columns(peer(d), k)],
            prod_recv.at[pl.ds(pl.multiple_of(source * block, block), block), columns(0, k)],
            p_ssem.at[k, d],
            p_rsem.at[k, source],
            peer(d),
        )

    def back_copy(k, d, source):
        return remote(
            b_send.at[pl.ds(pl.multiple_of(peer(d) * block, block), rows), columns(0, k)],
            b_recv.at[:, columns(source, k)],
            b_ssem.at[k, d],
            b_rsem.at[k, source],
            peer(d),
        )

    def short_copy(k, d, source):
        return remote(
            gs_send.at[:, columns(peer(d), k)],
            gs_recv.at[source, :, columns(0, k)],
            g_ssem.at[k, d],
            g_rsem.at[k, source],
            peer(d),
        )

    def scatter_copy(k, e, source):
        return remote(
            part.at[pl.ds(pl.multiple_of(mate(e) * EDGE, EDGE), EDGE), columns(0, k)],
            part_recv.at[source, :, columns(0, k)],
            r_ssem.at[k, e],
            r_rsem.at[k, source],
            me,
            mate(e),
        )

    def gather_copy(k, e, source):
        return remote(
            piece.at[:, columns(0, k)],
            gathered.at[pl.ds(pl.multiple_of(source * EDGE, EDGE), EDGE), columns(0, k)],
            a_ssem.at[k, e],
            a_rsem.at[k, source],
            me,
            mate(e),
        )

    def share_copy(k, e, source):
        return remote(
            gs_sum.at[:, columns(0, k)],
            gs_all.at[source, :, columns(0, k)],
            t_ssem.at[k, e],
            t_rsem.at[k, source],
            me,
            mate(e),
        )

    def out_copy(k, owner):
        return pltpu.make_async_copy(
            out_v.at[:, :, columns(owner, k)],
            out_ref.at[:, :, columns(owner, k)],
            out_sem.at[k, owner],
        )

    def products(k):
        for d in order + [0]:
            owner = peer(d)

            @pl.loop(0, tiles)
            def _(tile):
                inner = pl.ds(pl.multiple_of(k * width + tile * LANES, LANES), LANES)
                cols = pl.ds(pl.multiple_of(owner * own + k * width + tile * LANES, LANES), LANES)
                for s in range(2):
                    xf[s, :, cols] = xin[s, :, cols].astype(F32)
                    total = jnp.zeros((rows, LANES), F32)
                    for i in range(short_len):
                        total += sfull[owner, i, s : s + 1, inner] * xf[s, pl.ds(EDGE - i, rows), cols]
                    filt[s, :, cols] = total
                product = (filt[0, pl.ds(0, block), cols] * filt[1, pl.ds(0, block), cols]).astype(BF16)
                if d == 0:
                    prod_recv[pl.ds(pl.multiple_of(me * block, block), block), inner] = product
                else:
                    prod_send[:, cols] = product

            if d != 0:
                prod_copy(k, d, me).start()

    def medium(k):
        for d in order:
            prod_copy(k, d, peer(d)).wait_recv()
        cols = columns(0, k)
        fwd = fwd_ref[...]
        inv = inv_ref[...]
        skip = skip_ref[:, cols]

        def block_rows(f):
            return pl.ds(f * block, block)

        def dot(a, b):
            return jnp.dot(a, b, preferred_element_type=F32)

        response = dot(fwd, medium_ref[:, cols])
        for f in range(n):
            gspec[f] = dot(fwd, prod_recv[block_rows(f), cols])
        for f in range(n):
            zs[f] = gspec[f] + quarter_turn(gspec[f - 1]) if f else gspec[f]
        gain = jnp.zeros((1, width), F32)
        for f in range(n):
            product = prod_recv[block_rows(f), cols].astype(F32)
            mix = dot(inv, times(response, zs[f]).astype(BF16)) + skip * product
            weights = jnp.concatenate([wtile[block_rows(f), :]] * tiles, axis=1)
            grad = (weights * mix).astype(BF16)
            gmix[block_rows(f), :] = grad
            gain += jnp.sum(grad.astype(F32) * product, axis=0, keepdims=True)
        for f in range(n):
            gspec[f] = dot(fwd, gmix[block_rows(f), :])
        cross = jnp.zeros((2 * block, width), F32)
        for f in range(n):
            cross += times_conj(gspec[f], zs[f])
        for f in range(n):
            spec = gspec[f] - quarter_turn(gspec[f + 1]) if f < n - 1 else gspec[f]
            back = dot(inv, times_conj(spec, response).astype(BF16))
            back += skip * gmix[block_rows(f), :].astype(F32)
            b_send[block_rows(f), cols] = back.astype(BF16)
        for d in order:
            back_copy(k, d, me).start()
        high = cross.astype(BF16)
        low = (cross - high.astype(F32)).astype(BF16)
        taps = dot(inv, high) + dot(inv, low)
        if fused:
            part[:, cols] = taps.astype(BF16)
            for e in mates:
                scatter_copy(k, e, dp).start()
        else:
            taps_ref[:, cols] = taps
        gs_f[2 * short_len : 2 * short_len + 1, columns(me, k)] = gain

    def shorts(k):
        for d in [0] + order:
            owner = peer(d)
            if d != 0:
                back_copy(k, d, owner).wait_recv()

            @pl.loop(0, tiles)
            def _(tile):
                inner = pl.ds(pl.multiple_of(k * width + tile * LANES, LANES), LANES)
                cols = pl.ds(pl.multiple_of(owner * own + k * width + tile * LANES, LANES), LANES)
                if d == 0:
                    back = b_send[pl.ds(pl.multiple_of(me * block, block), rows), inner].astype(F32)
                else:
                    back = b_recv[:, cols].astype(F32)
                for s in range(2):
                    gbuf[s] = (back * filt[1 - s, :, cols]).astype(BF16).astype(F32)
                    total = jnp.zeros((block, LANES), F32)
                    grad = gbuf[s, pl.ds(0, block), :]
                    for i in range(short_len):
                        total += sfull[owner, i, s : s + 1, inner] * gbuf[s, pl.ds(i, block), :]
                        row = s * short_len + i
                        gs_f[row : row + 1, cols] = jnp.sum(
                            grad * xf[s, pl.ds(EDGE - i, block), cols], axis=0, keepdims=True
                        )
                    out_v[s, :, cols] = total.astype(BF16)

            out_copy(k, owner).start()
            if d != 0:
                gs_send[:, columns(owner, k)] = gs_f[:, columns(owner, k)].astype(BF16)
                short_copy(k, d, me).start()

    def reduce_taps(k):
        cols = columns(0, k)
        total = part[pl.ds(pl.multiple_of(dp * EDGE, EDGE), EDGE), cols].astype(F32)
        for e in mates:
            scatter_copy(k, e, mate(e)).wait_recv()
        for e in mates:
            total += part_recv[mate(e), :, cols].astype(F32)
        piece[:, cols] = total.astype(BF16)
        for e in mates:
            gather_copy(k, e, dp).start()
        gathered[pl.ds(pl.multiple_of(dp * EDGE, EDGE), EDGE), cols] = total.astype(BF16)

    def reduce_shorts(k):
        cols = columns(0, k)
        total = gs_f[:, columns(me, k)]
        for d in order:
            short_copy(k, d, peer(d)).wait_recv()
        for d in order:
            total += gs_recv[peer(d), :, cols].astype(F32)
        if fused:
            gs_sum[:, cols] = total.astype(BF16)
            for e in mates:
                share_copy(k, e, dp).start()
        else:
            write_shorts(cols, total)

    def write_shorts(cols, total):
        for s in range(2):
            for i in range(short_len):
                row = s * short_len + i
                short_out[i, s : s + 1, cols] = total[row : row + 1]
        gain_ref[:, cols] = total[2 * short_len : 2 * short_len + 1]

    @pl.loop(0, chunks + 2)
    def _(step):
        @pl.when(step < chunks)
        def _():
            products(step)

        @pl.when((step >= 1) & (step <= chunks))
        def _():
            medium(step - 1)

        if fused:

            @pl.when(step >= 2)
            def _():
                reduce_taps(step - 2)

        @pl.when(step >= 2)
        def _():
            shorts(step - 2)

        @pl.when(step >= 3)
        def _():
            reduce_shorts(step - 3)

    reduce_shorts(chunks - 1)

    @pl.loop(0, chunks)
    def _(k):
        for d in order:
            prod_copy(k, d, me).wait_send()
            back_copy(k, d, me).wait_send()
            short_copy(k, d, me).wait_send()
        for o in range(n):
            out_copy(k, o).wait()
        for e in mates:
            scatter_copy(k, e, dp).wait_send()
            gather_copy(k, e, dp).wait_send()
            share_copy(k, e, dp).wait_send()

    if fused:

        @pl.loop(0, chunks)
        def _(k):
            cols = columns(0, k)
            for e in mates:
                gather_copy(k, e, mate(e)).wait_recv()
            taps_ref[:, cols] = gathered[:, cols].astype(F32) / groups
            total = gs_sum[:, cols].astype(F32)
            for e in mates:
                share_copy(k, e, mate(e)).wait_recv()
            for e in mates:
                total += gs_all[mate(e), :, cols].astype(F32)
            write_shorts(cols, total / groups)

    for d in order:
        for copy in small_copies(d, me):
            copy.wait_send()

    @pl.when(me < n - 1)
    def _():
        to_later.wait_send()

    @pl.when(me > 0)
    def _():
        to_earlier.wait_send()


def local(projected, token_ids, short_filters, medium_filter, skip_gain):
    inputs = projected[:, 0]
    _, block, channels = inputs.shape
    short_len = short_filters.shape[1]
    own = medium_filter.shape[1]
    groups = lax.axis_size("dp")
    n = lax.axis_size("ctx")
    chunks = max(1, own // 256)
    width = own // chunks
    table = transform_table(block)
    forward = jnp.asarray(table.astype(ml_dtypes.bfloat16))
    inverse = jnp.asarray((table.T / block).astype(ml_dtypes.bfloat16))
    rows = block + EDGE
    vmem = pl.BlockSpec(memory_space=pltpu.VMEM)
    hbm = pl.BlockSpec(memory_space=pl.ANY)
    dma = pltpu.SemaphoreType.DMA
    fused = block == EDGE * groups
    held = groups if fused else 1
    out, taps, short, gain = pl.pallas_call(
        functools.partial(kernel, n, groups, chunks, fused),
        out_shape=(
            jax.ShapeDtypeStruct(inputs.shape, BF16),
            jax.ShapeDtypeStruct((block, own), F32),
            jax.ShapeDtypeStruct((short_len, 2, own), F32),
            jax.ShapeDtypeStruct((1, own), F32),
        ),
        in_specs=[hbm] * 7,
        out_specs=(hbm, vmem, vmem, vmem),
        scratch_shapes=[
            pltpu.VMEM((1, block), jnp.int32),
            pltpu.VMEM((block, own), BF16),
            pltpu.VMEM((1, own), F32),
            pltpu.VMEM((2 * block, block), BF16),
            pltpu.VMEM((block, 2 * block), BF16),
            pltpu.VMEM((block, own), BF16),
            pltpu.VMEM((held, EDGE, own), BF16),
            pltpu.VMEM((EDGE, own), BF16),
            pltpu.VMEM((block, own), BF16),
            pltpu.VMEM((EDGE, own), BF16),
            pltpu.VMEM((held, EDGE, own), BF16),
            pltpu.VMEM((2, block + 2 * EDGE, channels), BF16),
            pltpu.VMEM((2, block + 2 * EDGE, channels), F32),
            pltpu.VMEM((2, rows, channels), F32),
            pltpu.VMEM((n, short_len, 2, own), F32),
            pltpu.VMEM((n, 8, block), F32),
            pltpu.VMEM((n * block, LANES), F32),
            pltpu.VMEM((block, channels), BF16),
            pltpu.VMEM((n * block, own), BF16),
            pltpu.VMEM((n * block + EDGE, own), BF16),
            pltpu.VMEM((rows, channels), BF16),
            pltpu.VMEM((2, block, channels), BF16),
            pltpu.VMEM((2, rows, LANES), F32),
            pltpu.VMEM((EDGE, channels), F32),
            pltpu.VMEM((EDGE, channels), BF16),
            pltpu.VMEM((n, EDGE, own), BF16),
            pltpu.VMEM((n, 2 * block, width), F32),
            pltpu.VMEM((n, 2 * block, width), F32),
            pltpu.VMEM((n * block, width), BF16),
            dma((2,)),
            dma((2,)),
            dma((2, n)),
            dma((2, n)),
            dma((chunks, n)),
            dma((chunks, n)),
            dma((chunks, n)),
            dma((chunks, n)),
            dma((chunks, n)),
            dma((chunks, n)),
            dma((chunks, held)),
            dma((chunks, held)),
            dma((chunks, held)),
            dma((chunks, held)),
            dma((chunks, held)),
            dma((chunks, held)),
            dma((7,)),
            dma((chunks, n)),
        ],
        compiler_params=pltpu.CompilerParams(
            collective_id=0, has_side_effects=True, vmem_limit_bytes=60 * 1024 * 1024
        ),
    )(inputs, token_ids, short_filters.transpose(1, 0, 2), medium_filter, skip_gain[None], forward, inverse)
    if not fused:
        taps, short, gain = (
            lax.psum(part.astype(BF16), "dp").astype(F32) / groups for part in (taps, short, gain)
        )
    return out[:, None], short.transpose(1, 0, 2), taps, gain[0]


def solution(mesh):
    placed = (
        P(None, "dp", "ctx", None),
        P("dp", "ctx"),
        P(None, None, "ctx"),
        P(None, "ctx"),
        P("ctx"),
    )
    return jax.shard_map(
        local,
        mesh=mesh,
        in_specs=placed,
        out_specs=(P(None, "dp", "ctx", None), P(None, None, "ctx"), P(None, "ctx"), P("ctx")),
        check_vma=False,
    )
```

```python
import functools

import jax
import jax.numpy as jnp
import ml_dtypes
import numpy as np
from jax import lax
from jax.experimental import pallas as pl
from jax.experimental.pallas import tpu as pltpu
from jax.sharding import PartitionSpec as P

MESH = pl.DeviceIdType.MESH
F32 = jnp.float32
BF16 = jnp.bfloat16
LANES = 128
EDGE = 16


def transform_table(block):
    bins = np.concatenate([np.arange(0, block, 2), np.arange(1, block, 2)])
    angle = 2 * np.pi * np.outer(bins + 0.5, np.arange(block)) / (2 * block)
    return np.concatenate([np.cos(angle), -np.sin(angle)])


def quarter_turn(spec):
    half = spec.shape[0] // 4
    re_even, re_odd = spec[:half], spec[half : 2 * half]
    im_even, im_odd = spec[2 * half : 3 * half], spec[3 * half :]
    return jnp.concatenate([-im_even, im_odd, re_even, -re_odd], axis=0)


def times(a, b):
    half = a.shape[0] // 2
    ar, ai, br, bi = a[:half], a[half:], b[:half], b[half:]
    return jnp.concatenate([ar * br - ai * bi, ar * bi + ai * br], axis=0)


def times_conj(a, b):
    half = a.shape[0] // 2
    ar, ai, br, bi = a[:half], a[half:], b[:half], b[half:]
    return jnp.concatenate([ar * br + ai * bi, ai * br - ar * bi], axis=0)


def kernel(
    n,
    groups,
    chunks,
    fused,
    x_ref,
    tok_hbm,
    short_hbm,
    medium_hbm,
    skip_hbm,
    fwd_hbm,
    inv_hbm,
    out_ref,
    taps_ref,
    short_out,
    gain_ref,
    tok_ref,
    medium_ref,
    skip_ref,
    fwd_ref,
    inv_ref,
    part,
    part_recv,
    piece,
    gathered,
    gs_sum,
    gs_all,
    xin,
    xf,
    filt,
    sfull,
    wrow,
    wtile,
    prod_send,
    prod_recv,
    b_send,
    b_recv,
    out_v,
    gbuf,
    gs_f,
    gs_send,
    gs_recv,
    zs,
    gspec,
    gmix,
    edge_ssem,
    edge_rsem,
    halo_ssem,
    halo_rsem,
    weight_ssem,
    weight_rsem,
    small_ssem,
    small_rsem,
    p_ssem,
    p_rsem,
    b_ssem,
    b_rsem,
    g_ssem,
    g_rsem,
    r_ssem,
    r_rsem,
    a_ssem,
    a_rsem,
    t_ssem,
    t_rsem,
    in_sem,
    out_sem,
):
    me = lax.axis_index("ctx")
    dp = lax.axis_index("dp")
    block = x_ref.shape[1]
    own = medium_ref.shape[1]
    width = own // chunks
    tiles = width // LANES
    short_len = short_hbm.shape[0]
    rows = block + EDGE
    order = [d for d in (2, 1, 3) if d < n] + [d for d in range(4, n)]

    def peer(d):
        return lax.rem(me + d, n)

    def mate(e):
        return lax.rem(dp + e, groups)

    mates = range(1, groups) if fused else ()

    def remote(src, dst, ssem, rsem, to, group=None):
        return pltpu.make_async_remote_copy(
            src_ref=src,
            dst_ref=dst,
            send_sem=ssem,
            recv_sem=rsem,
            device_id=(dp if group is None else group, to),
            device_id_type=MESH,
        )

    loads = [
        pltpu.make_async_copy(src, dst, in_sem.at[j])
        for j, (src, dst) in enumerate(
            (
                (tok_hbm, tok_ref),
                (short_hbm, sfull.at[me]),
                (x_ref, xin.at[:, pl.ds(EDGE, block), :]),
                (medium_hbm, medium_ref),
                (skip_hbm, skip_ref),
                (fwd_hbm, fwd_ref),
                (inv_hbm, inv_ref),
            )
        )
    ]
    for load in loads:
        load.start()
    loads[0].wait()
    tokens = tok_ref[...]
    weight = jnp.where((tokens >= 97) & (tokens <= 122), 0.1, 1.0).astype(BF16).astype(F32)
    wrow[me] = jnp.broadcast_to(weight, (8, block))

    barrier = pltpu.get_barrier_semaphore()
    for d in order:
        pl.semaphore_signal(barrier, inc=1, device_id=(dp, peer(d)), device_id_type=MESH)
    for e in mates:
        pl.semaphore_signal(barrier, inc=1, device_id=(mate(e), me), device_id_type=MESH)
    pl.semaphore_wait(barrier, n - 1 + len(mates))

    later = lax.rem(me + 1, n)
    earlier = lax.rem(me + n - 1, n)

    def columns(owner, k):
        return pl.ds(pl.multiple_of(owner * own + k * width, LANES), width)

    def edge_copy(k, owner):
        return remote(
            x_ref.at[:, pl.ds(block - EDGE, EDGE), columns(owner, k)],
            xin.at[:, pl.ds(0, EDGE), columns(owner, k)],
            edge_ssem.at[k, owner],
            edge_rsem.at[k, owner],
            later,
        )

    to_earlier = remote(
        x_ref.at[:, pl.ds(0, EDGE), :],
        xin.at[:, pl.ds(block + EDGE, EDGE), :],
        halo_ssem,
        halo_rsem,
        earlier,
    )

    def filter_copy(k, d, source):
        return remote(
            sfull.at[source, :, :, columns(0, k)],
            sfull.at[source, :, :, columns(0, k)],
            small_ssem.at[k, d],
            small_rsem.at[k, source],
            peer(d),
        )

    def weight_copy(d, source):
        return remote(
            wrow.at[source],
            wrow.at[source],
            weight_ssem.at[d],
            weight_rsem.at[source],
            peer(d),
        )

    loads[1].wait()

    @pl.loop(0, chunks)
    def _(k):
        for d in order:
            filter_copy(k, d, me).start()

        @pl.when(me < n - 1)
        def _():
            for owner in range(n):
                edge_copy(k, owner).start()

    for d in order:
        weight_copy(d, me).start()

    @pl.when(me > 0)
    def _():
        to_earlier.start()

    zero_edge = jnp.zeros((2, EDGE, xin.shape[2]), BF16)

    @pl.when(me == 0)
    def _():
        xin[:, pl.ds(0, EDGE), :] = zero_edge

    @pl.when(me == n - 1)
    def _():
        xin[:, pl.ds(block + EDGE, EDGE), :] = zero_edge

    b_send[pl.ds(n * block, EDGE), :] = jnp.zeros((EDGE, own), BF16)
    gs_f[...] = jnp.zeros_like(gs_f)

    for load in loads[2:]:
        load.wait()

    def late_inputs():
        for d in order:
            weight_copy(d, peer(d)).wait_recv()
        for o in range(n):
            wtile[pl.ds(o * block, block), :] = jnp.broadcast_to(wrow[o, 0:1, :], (LANES, block)).T

        @pl.when(me < n - 1)
        def _():
            to_earlier.wait_recv()

    def prod_copy(k, d, source):
        return remote(
            prod_send.at[:, columns(peer(d), k)],
            prod_recv.at[pl.ds(pl.multiple_of(source * block, block), block), columns(0, k)],
            p_ssem.at[k, d],
            p_rsem.at[k, source],
            peer(d),
        )

    def back_copy(k, d, source):
        return remote(
            b_send.at[pl.ds(pl.multiple_of(peer(d) * block, block), rows), columns(0, k)],
            b_recv.at[:, columns(source, k)],
            b_ssem.at[k, d],
            b_rsem.at[k, source],
            peer(d),
        )

    def short_copy(k, d, source):
        return remote(
            gs_send.at[:, columns(peer(d), k)],
            gs_recv.at[source, :, columns(0, k)],
            g_ssem.at[k, d],
            g_rsem.at[k, source],
            peer(d),
        )

    def scatter_copy(k, e, source):
        return remote(
            part.at[pl.ds(pl.multiple_of(mate(e) * EDGE, EDGE), EDGE), columns(0, k)],
            part_recv.at[source, :, columns(0, k)],
            r_ssem.at[k, e],
            r_rsem.at[k, source],
            me,
            mate(e),
        )

    def gather_copy(k, e, source):
        return remote(
            piece.at[:, columns(0, k)],
            gathered.at[pl.ds(pl.multiple_of(source * EDGE, EDGE), EDGE), columns(0, k)],
            a_ssem.at[k, e],
            a_rsem.at[k, source],
            me,
            mate(e),
        )

    def share_copy(k, e, source):
        return remote(
            gs_sum.at[:, columns(0, k)],
            gs_all.at[source, :, columns(0, k)],
            t_ssem.at[k, e],
            t_rsem.at[k, source],
            me,
            mate(e),
        )

    def out_copy(k, owner):
        return pltpu.make_async_copy(
            out_v.at[:, :, columns(owner, k)],
            out_ref.at[:, :, columns(owner, k)],
            out_sem.at[k, owner],
        )

    def products(k):
        for d in order:
            filter_copy(k, d, peer(d)).wait_recv()

        @pl.when(me > 0)
        def _():
            for owner in range(n):
                edge_copy(k, owner).wait_recv()

        for d in order + [0]:
            owner = peer(d)

            @pl.loop(0, tiles)
            def _(tile):
                inner = pl.ds(pl.multiple_of(k * width + tile * LANES, LANES), LANES)
                cols = pl.ds(pl.multiple_of(owner * own + k * width + tile * LANES, LANES), LANES)
                for s in range(2):
                    xf[s, pl.ds(0, rows), cols] = xin[s, pl.ds(0, rows), cols].astype(F32)
                    total = jnp.zeros((block, LANES), F32)
                    for i in range(short_len):
                        total += sfull[owner, i, s : s + 1, inner] * xf[s, pl.ds(EDGE - i, block), cols]
                    filt[s, pl.ds(0, block), cols] = total
                product = (filt[0, pl.ds(0, block), cols] * filt[1, pl.ds(0, block), cols]).astype(BF16)
                if d == 0:
                    prod_recv[pl.ds(pl.multiple_of(me * block, block), block), inner] = product
                else:
                    prod_send[:, cols] = product

            if d != 0:
                prod_copy(k, d, me).start()

    def medium(k):
        for d in order:
            prod_copy(k, d, peer(d)).wait_recv()
        cols = columns(0, k)
        fwd = fwd_ref[...]
        inv = inv_ref[...]
        skip = skip_ref[:, cols]

        def block_rows(f):
            return pl.ds(f * block, block)

        def dot(a, b):
            return jnp.dot(a, b, preferred_element_type=F32)

        response = dot(fwd, medium_ref[:, cols])
        for f in range(n):
            gspec[f] = dot(fwd, prod_recv[block_rows(f), cols])
        for f in range(n):
            zs[f] = gspec[f] + quarter_turn(gspec[f - 1]) if f else gspec[f]
        gain = jnp.zeros((1, width), F32)
        for f in range(n):
            product = prod_recv[block_rows(f), cols].astype(F32)
            mix = dot(inv, times(response, zs[f]).astype(BF16)) + skip * product
            weights = jnp.concatenate([wtile[block_rows(f), :]] * tiles, axis=1)
            grad = (weights * mix).astype(BF16)
            gmix[block_rows(f), :] = grad
            gain += jnp.sum(grad.astype(F32) * product, axis=0, keepdims=True)
        for f in range(n):
            gspec[f] = dot(fwd, gmix[block_rows(f), :])
        cross = jnp.zeros((2 * block, width), F32)
        for f in range(n):
            cross += times_conj(gspec[f], zs[f])
        for f in range(n):
            spec = gspec[f] - quarter_turn(gspec[f + 1]) if f < n - 1 else gspec[f]
            back = dot(inv, times_conj(spec, response).astype(BF16))
            back += skip * gmix[block_rows(f), :].astype(F32)
            b_send[block_rows(f), cols] = back.astype(BF16)
        for d in order:
            back_copy(k, d, me).start()
        high = cross.astype(BF16)
        low = (cross - high.astype(F32)).astype(BF16)
        taps = dot(inv, high) + dot(inv, low)
        if fused:
            part[:, cols] = taps.astype(BF16)
            for e in mates:
                scatter_copy(k, e, dp).start()
        else:
            taps_ref[:, cols] = taps
        gs_f[2 * short_len : 2 * short_len + 1, columns(me, k)] = gain

    def shorts(k):
        for d in [0] + order:
            owner = peer(d)
            if d != 0:
                back_copy(k, d, owner).wait_recv()

            @pl.loop(0, tiles)
            def _(tile):
                inner = pl.ds(pl.multiple_of(k * width + tile * LANES, LANES), LANES)
                cols = pl.ds(pl.multiple_of(owner * own + k * width + tile * LANES, LANES), LANES)
                if d == 0:
                    back = b_send[pl.ds(pl.multiple_of(me * block, block), rows), inner].astype(F32)
                else:
                    back = b_recv[:, cols].astype(F32)
                for s in range(2):
                    xf[s, pl.ds(rows, EDGE), cols] = xin[s, pl.ds(rows, EDGE), cols].astype(F32)
                    total = jnp.zeros((EDGE, LANES), F32)
                    for i in range(short_len):
                        total += sfull[owner, i, s : s + 1, inner] * xf[s, pl.ds(rows - i, EDGE), cols]
                    filt[s, pl.ds(block, EDGE), cols] = total
                for s in range(2):
                    gbuf[s] = (back * filt[1 - s, :, cols]).astype(BF16).astype(F32)
                    total = jnp.zeros((block, LANES), F32)
                    grad = gbuf[s, pl.ds(0, block), :]
                    for i in range(short_len):
                        total += sfull[owner, i, s : s + 1, inner] * gbuf[s, pl.ds(i, block), :]
                        row = s * short_len + i
                        gs_f[row : row + 1, cols] = jnp.sum(
                            grad * xf[s, pl.ds(EDGE - i, block), cols], axis=0, keepdims=True
                        )
                    out_v[s, :, cols] = total.astype(BF16)

            out_copy(k, owner).start()
            if d != 0:
                gs_send[:, columns(owner, k)] = gs_f[:, columns(owner, k)].astype(BF16)
                short_copy(k, d, me).start()

    def reduce_taps(k):
        cols = columns(0, k)
        total = part[pl.ds(pl.multiple_of(dp * EDGE, EDGE), EDGE), cols].astype(F32)
        for e in mates:
            scatter_copy(k, e, mate(e)).wait_recv()
        for e in mates:
            total += part_recv[mate(e), :, cols].astype(F32)
        piece[:, cols] = total.astype(BF16)
        for e in mates:
            gather_copy(k, e, dp).start()
        gathered[pl.ds(pl.multiple_of(dp * EDGE, EDGE), EDGE), cols] = total.astype(BF16)

    def reduce_shorts(k):
        cols = columns(0, k)
        total = gs_f[:, columns(me, k)]
        for d in order:
            short_copy(k, d, peer(d)).wait_recv()
        for d in order:
            total += gs_recv[peer(d), :, cols].astype(F32)
        if fused:
            gs_sum[:, cols] = total.astype(BF16)
            for e in mates:
                share_copy(k, e, dp).start()
        else:
            write_shorts(cols, total)

    def write_shorts(cols, total):
        for s in range(2):
            for i in range(short_len):
                row = s * short_len + i
                short_out[i, s : s + 1, cols] = total[row : row + 1]
        gain_ref[:, cols] = total[2 * short_len : 2 * short_len + 1]

    ahead = min(2, chunks)
    back_lag = ahead + min(2, chunks)

    @pl.loop(0, chunks + back_lag)
    def _(step):
        @pl.when(step < chunks)
        def _():
            products(step)

        @pl.when(step == ahead)
        def _():
            late_inputs()

        @pl.when((step >= ahead) & (step < chunks + ahead))
        def _():
            medium(step - ahead)

        if fused:

            @pl.when(step >= back_lag)
            def _():
                reduce_taps(step - back_lag)

        @pl.when(step >= back_lag)
        def _():
            shorts(step - back_lag)

        @pl.when(step >= back_lag + 1)
        def _():
            reduce_shorts(step - back_lag - 1)

    reduce_shorts(chunks - 1)

    @pl.loop(0, chunks)
    def _(k):
        for d in order:
            prod_copy(k, d, me).wait_send()
            back_copy(k, d, me).wait_send()
            short_copy(k, d, me).wait_send()
            filter_copy(k, d, me).wait_send()
        for o in range(n):
            out_copy(k, o).wait()

        @pl.when(me < n - 1)
        def _():
            for owner in range(n):
                edge_copy(k, owner).wait_send()

        for e in mates:
            scatter_copy(k, e, dp).wait_send()
            gather_copy(k, e, dp).wait_send()
            share_copy(k, e, dp).wait_send()

    if fused:

        @pl.loop(0, chunks)
        def _(k):
            cols = columns(0, k)
            for e in mates:
                gather_copy(k, e, mate(e)).wait_recv()
            taps_ref[:, cols] = gathered[:, cols].astype(F32) / groups
            total = gs_sum[:, cols].astype(F32)
            for e in mates:
                share_copy(k, e, mate(e)).wait_recv()
            for e in mates:
                total += gs_all[mate(e), :, cols].astype(F32)
            write_shorts(cols, total / groups)

    for d in order:
        weight_copy(d, me).wait_send()

    @pl.when(me > 0)
    def _():
        to_earlier.wait_send()


def local(projected, token_ids, short_filters, medium_filter, skip_gain):
    inputs = projected[:, 0]
    _, block, channels = inputs.shape
    short_len = short_filters.shape[1]
    own = medium_filter.shape[1]
    groups = lax.axis_size("dp")
    n = lax.axis_size("ctx")
    chunks = max(1, own // 256)
    width = own // chunks
    table = transform_table(block)
    forward = jnp.asarray(table.astype(ml_dtypes.bfloat16))
    inverse = jnp.asarray((table.T / block).astype(ml_dtypes.bfloat16))
    rows = block + EDGE
    vmem = pl.BlockSpec(memory_space=pltpu.VMEM)
    hbm = pl.BlockSpec(memory_space=pl.ANY)
    dma = pltpu.SemaphoreType.DMA
    fused = block == EDGE * groups
    held = groups if fused else 1
    out, taps, short, gain = pl.pallas_call(
        functools.partial(kernel, n, groups, chunks, fused),
        out_shape=(
            jax.ShapeDtypeStruct(inputs.shape, BF16),
            jax.ShapeDtypeStruct((block, own), F32),
            jax.ShapeDtypeStruct((short_len, 2, own), F32),
            jax.ShapeDtypeStruct((1, own), F32),
        ),
        in_specs=[hbm] * 7,
        out_specs=(hbm, vmem, vmem, vmem),
        scratch_shapes=[
            pltpu.VMEM((1, block), jnp.int32),
            pltpu.VMEM((block, own), BF16),
            pltpu.VMEM((1, own), F32),
            pltpu.VMEM((2 * block, block), BF16),
            pltpu.VMEM((block, 2 * block), BF16),
            pltpu.VMEM((block, own), BF16),
            pltpu.VMEM((held, EDGE, own), BF16),
            pltpu.VMEM((EDGE, own), BF16),
            pltpu.VMEM((block, own), BF16),
            pltpu.VMEM((EDGE, own), BF16),
            pltpu.VMEM((held, EDGE, own), BF16),
            pltpu.VMEM((2, block + 2 * EDGE, channels), BF16),
            pltpu.VMEM((2, block + 2 * EDGE, channels), F32),
            pltpu.VMEM((2, rows, channels), F32),
            pltpu.VMEM((n, short_len, 2, own), F32),
            pltpu.VMEM((n, 8, block), F32),
            pltpu.VMEM((n * block, LANES), F32),
            pltpu.VMEM((block, channels), BF16),
            pltpu.VMEM((n * block, own), BF16),
            pltpu.VMEM((n * block + EDGE, own), BF16),
            pltpu.VMEM((rows, channels), BF16),
            pltpu.VMEM((2, block, channels), BF16),
            pltpu.VMEM((2, rows, LANES), F32),
            pltpu.VMEM((EDGE, channels), F32),
            pltpu.VMEM((EDGE, channels), BF16),
            pltpu.VMEM((n, EDGE, own), BF16),
            pltpu.VMEM((n, 2 * block, width), F32),
            pltpu.VMEM((n, 2 * block, width), F32),
            pltpu.VMEM((n * block, width), BF16),
            dma((chunks, n)),
            dma((chunks, n)),
            dma,
            dma,
            dma((n,)),
            dma((n,)),
            dma((chunks, n)),
            dma((chunks, n)),
            dma((chunks, n)),
            dma((chunks, n)),
            dma((chunks, n)),
            dma((chunks, n)),
            dma((chunks, n)),
            dma((chunks, n)),
            dma((chunks, held)),
            dma((chunks, held)),
            dma((chunks, held)),
            dma((chunks, held)),
            dma((chunks, held)),
            dma((chunks, held)),
            dma((7,)),
            dma((chunks, n)),
        ],
        compiler_params=pltpu.CompilerParams(
            collective_id=0, has_side_effects=True, vmem_limit_bytes=60 * 1024 * 1024
        ),
    )(inputs, token_ids, short_filters.transpose(1, 0, 2), medium_filter, skip_gain[None], forward, inverse)
    if not fused:
        taps, short, gain = (
            lax.psum(part.astype(BF16), "dp").astype(F32) / groups for part in (taps, short, gain)
        )
    return out[:, None], short.transpose(1, 0, 2), taps, gain[0]


def solution(mesh):
    placed = (
        P(None, "dp", "ctx", None),
        P("dp", "ctx"),
        P(None, None, "ctx"),
        P(None, "ctx"),
        P("ctx"),
    )
    return jax.shard_map(
        local,
        mesh=mesh,
        in_specs=placed,
        out_specs=(P(None, "dp", "ctx", None), P(None, None, "ctx"), P(None, "ctx"), P("ctx")),
        check_vma=False,
    )
```

```python
import functools

import jax
import jax.numpy as jnp
import ml_dtypes
import numpy as np
from jax import lax
from jax.experimental import pallas as pl
from jax.experimental.pallas import tpu as pltpu
from jax.sharding import PartitionSpec as P

MESH = pl.DeviceIdType.MESH
F32 = jnp.float32
BF16 = jnp.bfloat16
LANES = 128
EDGE = 16


def transform_table(block):
    bins = np.concatenate([np.arange(0, block, 2), np.arange(1, block, 2)])
    angle = 2 * np.pi * np.outer(bins + 0.5, np.arange(block)) / (2 * block)
    return np.concatenate([np.cos(angle), -np.sin(angle)])


def quarter_turn(spec):
    half = spec.shape[0] // 4
    re_even, re_odd = spec[:half], spec[half : 2 * half]
    im_even, im_odd = spec[2 * half : 3 * half], spec[3 * half :]
    return jnp.concatenate([-im_even, im_odd, re_even, -re_odd], axis=0)


def times(a, b):
    half = a.shape[0] // 2
    ar, ai, br, bi = a[:half], a[half:], b[:half], b[half:]
    return jnp.concatenate([ar * br - ai * bi, ar * bi + ai * br], axis=0)


def times_conj(a, b):
    half = a.shape[0] // 2
    ar, ai, br, bi = a[:half], a[half:], b[:half], b[half:]
    return jnp.concatenate([ar * br + ai * bi, ai * br - ar * bi], axis=0)


def kernel(
    n,
    groups,
    chunks,
    fused,
    x_ref,
    tok_hbm,
    short_hbm,
    medium_hbm,
    skip_hbm,
    fwd_hbm,
    inv_hbm,
    out_ref,
    taps_ref,
    short_out,
    gain_ref,
    tok_ref,
    medium_ref,
    skip_ref,
    fwd_ref,
    inv_ref,
    part,
    part_recv,
    piece,
    gathered,
    gs_sum,
    gs_all,
    xin,
    xf,
    filt,
    sfull,
    wrow,
    wtile,
    prod_send,
    prod_recv,
    b_send,
    b_recv,
    out_v,
    gbuf,
    gs_f,
    gs_send,
    gs_recv,
    zs,
    gspec,
    gmix,
    edge_ssem,
    edge_rsem,
    halo_ssem,
    halo_rsem,
    weight_ssem,
    weight_rsem,
    small_ssem,
    small_rsem,
    p_ssem,
    p_rsem,
    b_ssem,
    b_rsem,
    g_ssem,
    g_rsem,
    r_ssem,
    r_rsem,
    a_ssem,
    a_rsem,
    t_ssem,
    t_rsem,
    in_sem,
    out_sem,
):
    me = lax.axis_index("ctx")
    dp = lax.axis_index("dp")
    block = x_ref.shape[1]
    own = medium_ref.shape[1]
    width = own // chunks
    tiles = width // LANES
    short_len = short_hbm.shape[0]
    rows = block + EDGE
    order = [d for d in (2, 1, 3) if d < n] + [d for d in range(4, n)]

    def peer(d):
        return lax.rem(me + d, n)

    def mate(e):
        return lax.rem(dp + e, groups)

    mates = range(1, groups) if fused else ()

    def remote(src, dst, ssem, rsem, to, group=None):
        return pltpu.make_async_remote_copy(
            src_ref=src,
            dst_ref=dst,
            send_sem=ssem,
            recv_sem=rsem,
            device_id=(dp if group is None else group, to),
            device_id_type=MESH,
        )

    loads = [
        pltpu.make_async_copy(src, dst, in_sem.at[j])
        for j, (src, dst) in enumerate(
            (
                (tok_hbm, tok_ref),
                (short_hbm, sfull.at[me]),
                (x_ref, xin.at[:, pl.ds(EDGE, block), :]),
                (medium_hbm, medium_ref),
                (skip_hbm, skip_ref),
                (fwd_hbm, fwd_ref),
                (inv_hbm, inv_ref),
            )
        )
    ]
    for load in loads:
        load.start()
    loads[0].wait()
    tokens = tok_ref[...]
    weight = jnp.where((tokens >= 97) & (tokens <= 122), 0.1, 1.0).astype(BF16).astype(F32)
    wrow[me] = jnp.broadcast_to(weight, (8, block))

    barrier = pltpu.get_barrier_semaphore()
    for d in order:
        pl.semaphore_signal(barrier, inc=1, device_id=(dp, peer(d)), device_id_type=MESH)
    for e in mates:
        pl.semaphore_signal(barrier, inc=1, device_id=(mate(e), me), device_id_type=MESH)
    pl.semaphore_wait(barrier, n - 1 + len(mates))

    later = lax.rem(me + 1, n)
    earlier = lax.rem(me + n - 1, n)

    def columns(owner, k):
        return pl.ds(pl.multiple_of(owner * own + k * width, LANES), width)

    def edge_copy(k, owner):
        return remote(
            x_ref.at[:, pl.ds(block - EDGE, EDGE), columns(owner, k)],
            xin.at[:, pl.ds(0, EDGE), columns(owner, k)],
            edge_ssem.at[k, owner],
            edge_rsem.at[k, owner],
            later,
        )

    to_earlier = remote(
        x_ref.at[:, pl.ds(0, EDGE), :],
        xin.at[:, pl.ds(block + EDGE, EDGE), :],
        halo_ssem,
        halo_rsem,
        earlier,
    )

    def filter_copy(k, d, source):
        return remote(
            sfull.at[source, :, :, columns(0, k)],
            sfull.at[source, :, :, columns(0, k)],
            small_ssem.at[k, d],
            small_rsem.at[k, source],
            peer(d),
        )

    def weight_copy(d, source):
        return remote(
            wrow.at[source],
            wrow.at[source],
            weight_ssem.at[d],
            weight_rsem.at[source],
            peer(d),
        )

    loads[1].wait()

    @pl.loop(0, chunks)
    def _(k):
        for d in order:
            filter_copy(k, d, me).start()

        @pl.when(me < n - 1)
        def _():
            for owner in range(n):
                edge_copy(k, owner).start()

    for d in order:
        weight_copy(d, me).start()

    @pl.when(me > 0)
    def _():
        to_earlier.start()

    zero_edge = jnp.zeros((2, EDGE, xin.shape[2]), BF16)

    @pl.when(me == 0)
    def _():
        xin[:, pl.ds(0, EDGE), :] = zero_edge

    @pl.when(me == n - 1)
    def _():
        xin[:, pl.ds(block + EDGE, EDGE), :] = zero_edge

    b_send[pl.ds(n * block, EDGE), :] = jnp.zeros((EDGE, own), BF16)
    gs_f[...] = jnp.zeros_like(gs_f)

    for load in loads[2:]:
        load.wait()

    def late_inputs():
        for d in order:
            weight_copy(d, peer(d)).wait_recv()
        for o in range(n):
            wtile[pl.ds(o * block, block), :] = jnp.broadcast_to(wrow[o, 0:1, :], (LANES, block)).T

        @pl.when(me < n - 1)
        def _():
            to_earlier.wait_recv()

    def prod_copy(k, d, source):
        return remote(
            prod_send.at[:, columns(peer(d), k)],
            prod_recv.at[pl.ds(pl.multiple_of(source * block, block), block), columns(0, k)],
            p_ssem.at[k, d],
            p_rsem.at[k, source],
            peer(d),
        )

    def back_copy(k, d, source):
        return remote(
            b_send.at[pl.ds(pl.multiple_of(peer(d) * block, block), rows), columns(0, k)],
            b_recv.at[:, columns(source, k)],
            b_ssem.at[k, d],
            b_rsem.at[k, source],
            peer(d),
        )

    def short_copy(k, d, source):
        return remote(
            gs_send.at[:, columns(peer(d), k)],
            gs_recv.at[source, :, columns(0, k)],
            g_ssem.at[k, d],
            g_rsem.at[k, source],
            peer(d),
        )

    def scatter_copy(k, e, source):
        return remote(
            part.at[pl.ds(pl.multiple_of(mate(e) * EDGE, EDGE), EDGE), columns(0, k)],
            part_recv.at[source, :, columns(0, k)],
            r_ssem.at[k, e],
            r_rsem.at[k, source],
            me,
            mate(e),
        )

    def gather_copy(k, e, source):
        return remote(
            piece.at[:, columns(0, k)],
            gathered.at[pl.ds(pl.multiple_of(source * EDGE, EDGE), EDGE), columns(0, k)],
            a_ssem.at[k, e],
            a_rsem.at[k, source],
            me,
            mate(e),
        )

    def share_copy(k, e, source):
        return remote(
            gs_sum.at[:, columns(0, k)],
            gs_all.at[source, :, columns(0, k)],
            t_ssem.at[k, e],
            t_rsem.at[k, source],
            me,
            mate(e),
        )

    def out_copy(k, owner):
        return pltpu.make_async_copy(
            out_v.at[:, :, columns(owner, k)],
            out_ref.at[:, :, columns(owner, k)],
            out_sem.at[k, owner],
        )

    def products(k):
        for d in order:
            filter_copy(k, d, peer(d)).wait_recv()

        @pl.when(me > 0)
        def _():
            for owner in range(n):
                edge_copy(k, owner).wait_recv()

        for d in order + [0]:
            owner = peer(d)

            @pl.loop(0, tiles)
            def _(tile):
                inner = pl.ds(pl.multiple_of(k * width + tile * LANES, LANES), LANES)
                cols = pl.ds(pl.multiple_of(owner * own + k * width + tile * LANES, LANES), LANES)
                for s in range(2):
                    xf[s, pl.ds(0, rows), cols] = xin[s, pl.ds(0, rows), cols].astype(F32)
                    total = jnp.zeros((block, LANES), F32)
                    for i in range(short_len):
                        total += sfull[owner, i, s : s + 1, inner] * xf[s, pl.ds(EDGE - i, block), cols]
                    filt[s, pl.ds(0, block), cols] = total
                product = (filt[0, pl.ds(0, block), cols] * filt[1, pl.ds(0, block), cols]).astype(BF16)
                if d == 0:
                    prod_recv[pl.ds(pl.multiple_of(me * block, block), block), inner] = product
                else:
                    prod_send[:, cols] = product

            if d != 0:
                prod_copy(k, d, me).start()

    def medium(k):
        for d in order:
            prod_copy(k, d, peer(d)).wait_recv()
        cols = columns(0, k)
        fwd = fwd_ref[...]
        inv = inv_ref[...]
        skip = skip_ref[:, cols]

        def block_rows(f):
            return pl.ds(f * block, block)

        def dot(a, b):
            return jnp.dot(a, b, preferred_element_type=F32)

        response = dot(fwd, medium_ref[:, cols])
        for f in range(n):
            gspec[f] = dot(fwd, prod_recv[block_rows(f), cols])
        for f in range(n):
            zs[f] = gspec[f] + quarter_turn(gspec[f - 1]) if f else gspec[f]
        gain = jnp.zeros((1, width), F32)
        for f in range(n):
            product = prod_recv[block_rows(f), cols].astype(F32)
            mix = dot(inv, times(response, zs[f]).astype(BF16)) + skip * product
            weights = jnp.concatenate([wtile[block_rows(f), :]] * tiles, axis=1)
            grad = (weights * mix).astype(BF16)
            gmix[block_rows(f), :] = grad
            gain += jnp.sum(grad.astype(F32) * product, axis=0, keepdims=True)
        for f in range(n):
            gspec[f] = dot(fwd, gmix[block_rows(f), :])
        cross = jnp.zeros((2 * block, width), F32)
        for f in range(n):
            cross += times_conj(gspec[f], zs[f])
        for f in range(n):
            spec = gspec[f] - quarter_turn(gspec[f + 1]) if f < n - 1 else gspec[f]
            back = dot(inv, times_conj(spec, response).astype(BF16))
            back += skip * gmix[block_rows(f), :].astype(F32)
            b_send[block_rows(f), cols] = back.astype(BF16)
        for d in order:
            back_copy(k, d, me).start()
        high = cross.astype(BF16)
        low = (cross - high.astype(F32)).astype(BF16)
        taps = dot(inv, high) + dot(inv, low)
        if fused:
            part[:, cols] = taps.astype(BF16)
            for e in mates:
                scatter_copy(k, e, dp).start()
        else:
            taps_ref[:, cols] = taps
        gs_f[2 * short_len : 2 * short_len + 1, columns(me, k)] = gain

    def shorts(k):
        for d in [0] + order:
            owner = peer(d)
            if d != 0:
                back_copy(k, d, owner).wait_recv()

            @pl.loop(0, tiles)
            def _(tile):
                inner = pl.ds(pl.multiple_of(k * width + tile * LANES, LANES), LANES)
                cols = pl.ds(pl.multiple_of(owner * own + k * width + tile * LANES, LANES), LANES)
                if d == 0:
                    back = b_send[pl.ds(pl.multiple_of(me * block, block), rows), inner].astype(F32)
                else:
                    back = b_recv[:, cols].astype(F32)
                for s in range(2):
                    xf[s, pl.ds(rows, EDGE), cols] = xin[s, pl.ds(rows, EDGE), cols].astype(F32)
                    total = jnp.zeros((EDGE, LANES), F32)
                    for i in range(short_len):
                        total += sfull[owner, i, s : s + 1, inner] * xf[s, pl.ds(rows - i, EDGE), cols]
                    filt[s, pl.ds(block, EDGE), cols] = total
                for s in range(2):
                    gbuf[s] = (back * filt[1 - s, :, cols]).astype(BF16).astype(F32)
                    total = jnp.zeros((block, LANES), F32)
                    grad = gbuf[s, pl.ds(0, block), :]
                    for i in range(short_len):
                        total += sfull[owner, i, s : s + 1, inner] * gbuf[s, pl.ds(i, block), :]
                        row = s * short_len + i
                        gs_f[row : row + 1, cols] = jnp.sum(
                            grad * xf[s, pl.ds(EDGE - i, block), cols], axis=0, keepdims=True
                        )
                    out_v[s, :, cols] = total.astype(BF16)

            out_copy(k, owner).start()
            if d != 0:
                gs_send[:, columns(owner, k)] = gs_f[:, columns(owner, k)].astype(BF16)
                short_copy(k, d, me).start()

    def reduce_taps(k):
        cols = columns(0, k)
        total = part[pl.ds(pl.multiple_of(dp * EDGE, EDGE), EDGE), cols].astype(F32)
        for e in mates:
            scatter_copy(k, e, mate(e)).wait_recv()
        for e in mates:
            total += part_recv[mate(e), :, cols].astype(F32)
        piece[:, cols] = total.astype(BF16)
        for e in mates:
            gather_copy(k, e, dp).start()
        gathered[pl.ds(pl.multiple_of(dp * EDGE, EDGE), EDGE), cols] = total.astype(BF16)

    def reduce_shorts(k):
        cols = columns(0, k)
        total = gs_f[:, columns(me, k)]
        for d in order:
            short_copy(k, d, peer(d)).wait_recv()
        for d in order:
            total += gs_recv[peer(d), :, cols].astype(F32)
        if fused:
            gs_sum[:, cols] = total.astype(BF16)
            for e in mates:
                share_copy(k, e, dp).start()
        else:
            write_shorts(cols, total)

    def write_shorts(cols, total):
        for s in range(2):
            for i in range(short_len):
                row = s * short_len + i
                short_out[i, s : s + 1, cols] = total[row : row + 1]
        gain_ref[:, cols] = total[2 * short_len : 2 * short_len + 1]

    ahead = min(2, chunks)
    back_lag = ahead + min(2, chunks)

    @pl.loop(0, chunks + back_lag)
    def _(step):
        @pl.when(step < chunks)
        def _():
            products(step)

        @pl.when(step == ahead)
        def _():
            late_inputs()

        @pl.when((step >= ahead) & (step < chunks + ahead))
        def _():
            medium(step - ahead)

        if fused:

            @pl.when(step >= back_lag)
            def _():
                reduce_taps(step - back_lag)

        @pl.when(step >= back_lag)
        def _():
            shorts(step - back_lag)

        @pl.when(step >= back_lag + 1)
        def _():
            reduce_shorts(step - back_lag - 1)

    reduce_shorts(chunks - 1)

    @pl.loop(0, chunks)
    def _(k):
        for d in order:
            prod_copy(k, d, me).wait_send()
            back_copy(k, d, me).wait_send()
            short_copy(k, d, me).wait_send()
            filter_copy(k, d, me).wait_send()
        for o in range(n):
            out_copy(k, o).wait()

        @pl.when(me < n - 1)
        def _():
            for owner in range(n):
                edge_copy(k, owner).wait_send()

        for e in mates:
            scatter_copy(k, e, dp).wait_send()
            gather_copy(k, e, dp).wait_send()
            share_copy(k, e, dp).wait_send()

    if fused:

        @pl.loop(0, chunks)
        def _(k):
            cols = columns(0, k)
            for e in mates:
                gather_copy(k, e, mate(e)).wait_recv()
            taps_ref[:, cols] = gathered[:, cols].astype(F32) / groups
            total = gs_sum[:, cols].astype(F32)
            for e in mates:
                share_copy(k, e, mate(e)).wait_recv()
            for e in mates:
                total += gs_all[mate(e), :, cols].astype(F32)
            write_shorts(cols, total / groups)

    for d in order:
        weight_copy(d, me).wait_send()

    @pl.when(me > 0)
    def _():
        to_earlier.wait_send()


def local(projected, token_ids, short_filters, medium_filter, skip_gain):
    inputs = projected[:, 0]
    _, block, channels = inputs.shape
    short_len = short_filters.shape[1]
    own = medium_filter.shape[1]
    groups = lax.axis_size("dp")
    n = lax.axis_size("ctx")
    chunks = max(1, own // 512)
    width = own // chunks
    table = transform_table(block)
    forward = jnp.asarray(table.astype(ml_dtypes.bfloat16))
    inverse = jnp.asarray((table.T / block).astype(ml_dtypes.bfloat16))
    rows = block + EDGE
    vmem = pl.BlockSpec(memory_space=pltpu.VMEM)
    hbm = pl.BlockSpec(memory_space=pl.ANY)
    dma = pltpu.SemaphoreType.DMA
    fused = block == EDGE * groups
    held = groups if fused else 1
    out, taps, short, gain = pl.pallas_call(
        functools.partial(kernel, n, groups, chunks, fused),
        out_shape=(
            jax.ShapeDtypeStruct(inputs.shape, BF16),
            jax.ShapeDtypeStruct((block, own), F32),
            jax.ShapeDtypeStruct((short_len, 2, own), F32),
            jax.ShapeDtypeStruct((1, own), F32),
        ),
        in_specs=[hbm] * 7,
        out_specs=(hbm, vmem, vmem, vmem),
        scratch_shapes=[
            pltpu.VMEM((1, block), jnp.int32),
            pltpu.VMEM((block, own), BF16),
            pltpu.VMEM((1, own), F32),
            pltpu.VMEM((2 * block, block), BF16),
            pltpu.VMEM((block, 2 * block), BF16),
            pltpu.VMEM((block, own), BF16),
            pltpu.VMEM((held, EDGE, own), BF16),
            pltpu.VMEM((EDGE, own), BF16),
            pltpu.VMEM((block, own), BF16),
            pltpu.VMEM((EDGE, own), BF16),
            pltpu.VMEM((held, EDGE, own), BF16),
            pltpu.VMEM((2, block + 2 * EDGE, channels), BF16),
            pltpu.VMEM((2, block + 2 * EDGE, channels), F32),
            pltpu.VMEM((2, rows, channels), F32),
            pltpu.VMEM((n, short_len, 2, own), F32),
            pltpu.VMEM((n, 8, block), F32),
            pltpu.VMEM((n * block, LANES), F32),
            pltpu.VMEM((block, channels), BF16),
            pltpu.VMEM((n * block, own), BF16),
            pltpu.VMEM((n * block + EDGE, own), BF16),
            pltpu.VMEM((rows, channels), BF16),
            pltpu.VMEM((2, block, channels), BF16),
            pltpu.VMEM((2, rows, LANES), F32),
            pltpu.VMEM((EDGE, channels), F32),
            pltpu.VMEM((EDGE, channels), BF16),
            pltpu.VMEM((n, EDGE, own), BF16),
            pltpu.VMEM((n, 2 * block, width), F32),
            pltpu.VMEM((n, 2 * block, width), F32),
            pltpu.VMEM((n * block, width), BF16),
            dma((chunks, n)),
            dma((chunks, n)),
            dma,
            dma,
            dma((n,)),
            dma((n,)),
            dma((chunks, n)),
            dma((chunks, n)),
            dma((chunks, n)),
            dma((chunks, n)),
            dma((chunks, n)),
            dma((chunks, n)),
            dma((chunks, n)),
            dma((chunks, n)),
            dma((chunks, held)),
            dma((chunks, held)),
            dma((chunks, held)),
            dma((chunks, held)),
            dma((chunks, held)),
            dma((chunks, held)),
            dma((7,)),
            dma((chunks, n)),
        ],
        compiler_params=pltpu.CompilerParams(
            collective_id=0, has_side_effects=True, vmem_limit_bytes=60 * 1024 * 1024
        ),
    )(inputs, token_ids, short_filters.transpose(1, 0, 2), medium_filter, skip_gain[None], forward, inverse)
    if not fused:
        taps, short, gain = (
            lax.psum(part.astype(BF16), "dp").astype(F32) / groups for part in (taps, short, gain)
        )
    return out[:, None], short.transpose(1, 0, 2), taps, gain[0]


def solution(mesh):
    placed = (
        P(None, "dp", "ctx", None),
        P("dp", "ctx"),
        P(None, None, "ctx"),
        P(None, "ctx"),
        P("ctx"),
    )
    return jax.shard_map(
        local,
        mesh=mesh,
        in_specs=placed,
        out_specs=(P(None, "dp", "ctx", None), P(None, None, "ctx"), P(None, "ctx"), P("ctx")),
        check_vma=False,
    )
```

```python
import functools

import jax
import jax.numpy as jnp
import ml_dtypes
import numpy as np
from jax import lax
from jax.experimental import pallas as pl
from jax.experimental.pallas import tpu as pltpu
from jax.sharding import PartitionSpec as P

MESH = pl.DeviceIdType.MESH
F32 = jnp.float32
BF16 = jnp.bfloat16
LANES = 128
EDGE = 16


def transform_table(block):
    bins = np.concatenate([np.arange(0, block, 2), np.arange(1, block, 2)])
    angle = 2 * np.pi * np.outer(bins + 0.5, np.arange(block)) / (2 * block)
    return np.concatenate([np.cos(angle), -np.sin(angle)])


def quarter_turn(spec):
    half = spec.shape[0] // 4
    re_even, re_odd = spec[:half], spec[half : 2 * half]
    im_even, im_odd = spec[2 * half : 3 * half], spec[3 * half :]
    return jnp.concatenate([-im_even, im_odd, re_even, -re_odd], axis=0)


def times(a, b):
    half = a.shape[0] // 2
    ar, ai, br, bi = a[:half], a[half:], b[:half], b[half:]
    return jnp.concatenate([ar * br - ai * bi, ar * bi + ai * br], axis=0)


def times_conj(a, b):
    half = a.shape[0] // 2
    ar, ai, br, bi = a[:half], a[half:], b[:half], b[half:]
    return jnp.concatenate([ar * br + ai * bi, ai * br - ar * bi], axis=0)


def kernel(
    n,
    groups,
    chunks,
    fused,
    x_ref,
    tok_hbm,
    short_hbm,
    medium_hbm,
    skip_hbm,
    fwd_hbm,
    inv_hbm,
    out_ref,
    taps_ref,
    short_out,
    gain_ref,
    tok_ref,
    medium_ref,
    skip_ref,
    fwd_ref,
    inv_ref,
    part,
    part_recv,
    piece,
    gathered,
    gs_sum,
    gs_all,
    xin,
    xf,
    filt,
    sfull,
    wrow,
    wtile,
    prod_send,
    prod_recv,
    b_send,
    b_recv,
    out_v,
    gbuf,
    gs_f,
    gs_send,
    gs_recv,
    zs,
    gspec,
    gmix,
    edge_ssem,
    edge_rsem,
    halo_ssem,
    halo_rsem,
    weight_ssem,
    weight_rsem,
    small_ssem,
    small_rsem,
    p_ssem,
    p_rsem,
    b_ssem,
    b_rsem,
    g_ssem,
    g_rsem,
    r_ssem,
    r_rsem,
    a_ssem,
    a_rsem,
    t_ssem,
    t_rsem,
    in_sem,
    out_sem,
):
    me = lax.axis_index("ctx")
    dp = lax.axis_index("dp")
    block = x_ref.shape[1]
    own = medium_ref.shape[1]
    width = own // chunks
    tiles = width // LANES
    short_len = short_hbm.shape[0]
    rows = block + EDGE
    order = [d for d in (2, 1, 3) if d < n] + [d for d in range(4, n)]

    def peer(d):
        return lax.rem(me + d, n)

    def mate(e):
        return lax.rem(dp + e, groups)

    mates = range(1, groups) if fused else ()

    def remote(src, dst, ssem, rsem, to, group=None):
        return pltpu.make_async_remote_copy(
            src_ref=src,
            dst_ref=dst,
            send_sem=ssem,
            recv_sem=rsem,
            device_id=(dp if group is None else group, to),
            device_id_type=MESH,
        )

    loads = [
        pltpu.make_async_copy(src, dst, in_sem.at[j])
        for j, (src, dst) in enumerate(
            (
                (tok_hbm, tok_ref),
                (short_hbm, sfull.at[me]),
                (x_ref, xin.at[:, pl.ds(EDGE, block), :]),
                (medium_hbm, medium_ref),
                (skip_hbm, skip_ref),
                (fwd_hbm, fwd_ref),
                (inv_hbm, inv_ref),
            )
        )
    ]
    for load in loads:
        load.start()
    loads[0].wait()
    tokens = tok_ref[...]
    weight = jnp.where((tokens >= 97) & (tokens <= 122), 0.1, 1.0).astype(BF16).astype(F32)
    wrow[me] = jnp.broadcast_to(weight, (8, block))

    barrier = pltpu.get_barrier_semaphore()
    for d in order:
        pl.semaphore_signal(barrier, inc=1, device_id=(dp, peer(d)), device_id_type=MESH)
    for e in mates:
        pl.semaphore_signal(barrier, inc=1, device_id=(mate(e), me), device_id_type=MESH)
    pl.semaphore_wait(barrier, n - 1 + len(mates))

    later = lax.rem(me + 1, n)
    earlier = lax.rem(me + n - 1, n)

    def columns(owner, k):
        return pl.ds(pl.multiple_of(owner * own + k * width, LANES), width)

    def edge_copy(k, owner):
        return remote(
            x_ref.at[:, pl.ds(block - EDGE, EDGE), columns(owner, k)],
            xin.at[:, pl.ds(0, EDGE), columns(owner, k)],
            edge_ssem.at[k, owner],
            edge_rsem.at[k, owner],
            later,
        )

    to_earlier = remote(
        x_ref.at[:, pl.ds(0, EDGE), :],
        xin.at[:, pl.ds(block + EDGE, EDGE), :],
        halo_ssem,
        halo_rsem,
        earlier,
    )

    def filter_copy(k, d, source):
        return remote(
            sfull.at[source, :, :, columns(0, k)],
            sfull.at[source, :, :, columns(0, k)],
            small_ssem.at[k, d],
            small_rsem.at[k, source],
            peer(d),
        )

    def weight_copy(d, source):
        return remote(
            wrow.at[source],
            wrow.at[source],
            weight_ssem.at[d],
            weight_rsem.at[source],
            peer(d),
        )

    loads[1].wait()

    @pl.loop(0, chunks)
    def _(k):
        for d in order:
            filter_copy(k, d, me).start()

        @pl.when(me < n - 1)
        def _():
            for owner in range(n):
                edge_copy(k, owner).start()

    for d in order:
        weight_copy(d, me).start()

    @pl.when(me > 0)
    def _():
        to_earlier.start()

    zero_edge = jnp.zeros((2, EDGE, xin.shape[2]), BF16)

    @pl.when(me == 0)
    def _():
        xin[:, pl.ds(0, EDGE), :] = zero_edge

    @pl.when(me == n - 1)
    def _():
        xin[:, pl.ds(block + EDGE, EDGE), :] = zero_edge

    b_send[pl.ds(n * block, EDGE), :] = jnp.zeros((EDGE, own), BF16)
    gs_f[...] = jnp.zeros_like(gs_f)

    for load in loads[2:]:
        load.wait()

    def late_inputs():
        for d in order:
            weight_copy(d, peer(d)).wait_recv()
        for o in range(n):
            wtile[pl.ds(o * block, block), :] = jnp.broadcast_to(wrow[o, 0:1, :], (LANES, block)).T

        @pl.when(me < n - 1)
        def _():
            to_earlier.wait_recv()

    def prod_copy(k, d, source):
        return remote(
            prod_send.at[:, columns(peer(d), k)],
            prod_recv.at[pl.ds(pl.multiple_of(source * block, block), block), columns(0, k)],
            p_ssem.at[k, d],
            p_rsem.at[k, source],
            peer(d),
        )

    def back_copy(k, d, source):
        return remote(
            b_send.at[pl.ds(pl.multiple_of(peer(d) * block, block), rows), columns(0, k)],
            b_recv.at[:, columns(source, k)],
            b_ssem.at[k, d],
            b_rsem.at[k, source],
            peer(d),
        )

    def short_copy(k, d, source):
        return remote(
            gs_send.at[:, columns(peer(d), k)],
            gs_recv.at[source, :, columns(0, k)],
            g_ssem.at[k, d],
            g_rsem.at[k, source],
            peer(d),
        )

    def scatter_copy(k, e, source):
        return remote(
            part.at[pl.ds(pl.multiple_of(mate(e) * EDGE, EDGE), EDGE), columns(0, k)],
            part_recv.at[source, :, columns(0, k)],
            r_ssem.at[k, e],
            r_rsem.at[k, source],
            me,
            mate(e),
        )

    def gather_copy(k, e, source):
        return remote(
            piece.at[:, columns(0, k)],
            gathered.at[pl.ds(pl.multiple_of(source * EDGE, EDGE), EDGE), columns(0, k)],
            a_ssem.at[k, e],
            a_rsem.at[k, source],
            me,
            mate(e),
        )

    def share_copy(k, e, source):
        return remote(
            gs_sum.at[:, columns(0, k)],
            gs_all.at[source, :, columns(0, k)],
            t_ssem.at[k, e],
            t_rsem.at[k, source],
            me,
            mate(e),
        )

    def out_copy(k, owner):
        return pltpu.make_async_copy(
            out_v.at[:, :, columns(owner, k)],
            out_ref.at[:, :, columns(owner, k)],
            out_sem.at[k, owner],
        )

    def products(k):
        for d in order:
            filter_copy(k, d, peer(d)).wait_recv()

        @pl.when(me > 0)
        def _():
            for owner in range(n):
                edge_copy(k, owner).wait_recv()

        for d in order + [0]:
            owner = peer(d)

            @pl.loop(0, tiles)
            def _(tile):
                inner = pl.ds(pl.multiple_of(k * width + tile * LANES, LANES), LANES)
                cols = pl.ds(pl.multiple_of(owner * own + k * width + tile * LANES, LANES), LANES)
                for s in range(2):
                    xf[s, pl.ds(0, rows), cols] = xin[s, pl.ds(0, rows), cols].astype(F32)
                    total = jnp.zeros((block, LANES), F32)
                    for i in range(short_len):
                        total += sfull[owner, i, s : s + 1, inner] * xf[s, pl.ds(EDGE - i, block), cols]
                    filt[s, pl.ds(0, block), cols] = total
                product = (filt[0, pl.ds(0, block), cols] * filt[1, pl.ds(0, block), cols]).astype(BF16)
                if d == 0:
                    prod_recv[pl.ds(pl.multiple_of(me * block, block), block), inner] = product
                else:
                    prod_send[:, cols] = product

            if d != 0:
                prod_copy(k, d, me).start()

    def medium(k):
        for d in order:
            prod_copy(k, d, peer(d)).wait_recv()
        cols = columns(0, k)
        fwd = fwd_ref[...]
        inv = inv_ref[...]
        skip = skip_ref[:, cols]

        def block_rows(f):
            return pl.ds(f * block, block)

        def dot(a, b):
            return jnp.dot(a, b, preferred_element_type=F32)

        response = dot(fwd, medium_ref[:, cols])
        for f in range(n):
            gspec[f] = dot(fwd, prod_recv[block_rows(f), cols])
        for f in range(n):
            zs[f] = gspec[f] + quarter_turn(gspec[f - 1]) if f else gspec[f]
        gain = jnp.zeros((1, width), F32)
        for f in range(n):
            product = prod_recv[block_rows(f), cols].astype(F32)
            mix = dot(inv, times(response, zs[f]).astype(BF16)) + skip * product
            weights = jnp.concatenate([wtile[block_rows(f), :]] * tiles, axis=1)
            grad = (weights * mix).astype(BF16)
            gmix[block_rows(f), :] = grad
            gain += jnp.sum(grad.astype(F32) * product, axis=0, keepdims=True)
        for f in range(n):
            gspec[f] = dot(fwd, gmix[block_rows(f), :])
        cross = jnp.zeros((2 * block, width), F32)
        for f in range(n):
            cross += times_conj(gspec[f], zs[f])
        for f in range(n):
            spec = gspec[f] - quarter_turn(gspec[f + 1]) if f < n - 1 else gspec[f]
            back = dot(inv, times_conj(spec, response).astype(BF16))
            back += skip * gmix[block_rows(f), :].astype(F32)
            b_send[block_rows(f), cols] = back.astype(BF16)
        for d in order:
            back_copy(k, d, me).start()
        high = cross.astype(BF16)
        low = (cross - high.astype(F32)).astype(BF16)
        taps = dot(inv, high) + dot(inv, low)
        if fused:
            part[:, cols] = taps.astype(BF16)
            for e in mates:
                scatter_copy(k, e, dp).start()
        else:
            taps_ref[:, cols] = taps
        gs_f[2 * short_len : 2 * short_len + 1, columns(me, k)] = gain

    def shorts(k):
        for d in [0] + order:
            owner = peer(d)
            if d != 0:
                back_copy(k, d, owner).wait_recv()

            @pl.loop(0, tiles)
            def _(tile):
                inner = pl.ds(pl.multiple_of(k * width + tile * LANES, LANES), LANES)
                cols = pl.ds(pl.multiple_of(owner * own + k * width + tile * LANES, LANES), LANES)
                if d == 0:
                    back = b_send[pl.ds(pl.multiple_of(me * block, block), rows), inner].astype(F32)
                else:
                    back = b_recv[:, cols].astype(F32)
                for s in range(2):
                    xf[s, pl.ds(rows, EDGE), cols] = xin[s, pl.ds(rows, EDGE), cols].astype(F32)
                    total = jnp.zeros((EDGE, LANES), F32)
                    for i in range(short_len):
                        total += sfull[owner, i, s : s + 1, inner] * xf[s, pl.ds(rows - i, EDGE), cols]
                    filt[s, pl.ds(block, EDGE), cols] = total
                for s in range(2):
                    gbuf[s] = (back * filt[1 - s, :, cols]).astype(BF16).astype(F32)
                    total = jnp.zeros((block, LANES), F32)
                    grad = gbuf[s, pl.ds(0, block), :]
                    for i in range(short_len):
                        total += sfull[owner, i, s : s + 1, inner] * gbuf[s, pl.ds(i, block), :]
                        row = s * short_len + i
                        gs_f[row : row + 1, cols] = jnp.sum(
                            grad * xf[s, pl.ds(EDGE - i, block), cols], axis=0, keepdims=True
                        )
                    out_v[s, :, cols] = total.astype(BF16)

            out_copy(k, owner).start()
            if d != 0:
                gs_send[:, columns(owner, k)] = gs_f[:, columns(owner, k)].astype(BF16)
                short_copy(k, d, me).start()

    def reduce_taps(k):
        cols = columns(0, k)
        total = part[pl.ds(pl.multiple_of(dp * EDGE, EDGE), EDGE), cols].astype(F32)
        for e in mates:
            scatter_copy(k, e, mate(e)).wait_recv()
        for e in mates:
            total += part_recv[mate(e), :, cols].astype(F32)
        piece[:, cols] = total.astype(BF16)
        for e in mates:
            gather_copy(k, e, dp).start()
        gathered[pl.ds(pl.multiple_of(dp * EDGE, EDGE), EDGE), cols] = total.astype(BF16)

    def reduce_shorts(k):
        cols = columns(0, k)
        total = gs_f[:, columns(me, k)]
        for d in order:
            short_copy(k, d, peer(d)).wait_recv()
        for d in order:
            total += gs_recv[peer(d), :, cols].astype(F32)
        if fused:
            gs_sum[:, cols] = total.astype(BF16)
            for e in mates:
                share_copy(k, e, dp).start()
        else:
            write_shorts(cols, total)

    def write_shorts(cols, total):
        for s in range(2):
            for i in range(short_len):
                row = s * short_len + i
                short_out[i, s : s + 1, cols] = total[row : row + 1]
        gain_ref[:, cols] = total[2 * short_len : 2 * short_len + 1]

    ahead = min(2, chunks)
    back_lag = ahead + min(2, chunks)

    @pl.loop(0, chunks + back_lag)
    def _(step):
        @pl.when(step < chunks)
        def _():
            products(step)

        @pl.when(step == ahead)
        def _():
            late_inputs()

        @pl.when((step >= ahead) & (step < chunks + ahead))
        def _():
            medium(step - ahead)

        if fused:

            @pl.when(step >= back_lag)
            def _():
                reduce_taps(step - back_lag)

        @pl.when(step >= back_lag + 1)
        def _():
            reduce_shorts(step - back_lag - 1)

        @pl.when(step >= back_lag)
        def _():
            shorts(step - back_lag)

    reduce_shorts(chunks - 1)

    @pl.loop(0, chunks)
    def _(k):
        for d in order:
            prod_copy(k, d, me).wait_send()
            back_copy(k, d, me).wait_send()
            short_copy(k, d, me).wait_send()
            filter_copy(k, d, me).wait_send()
        for o in range(n):
            out_copy(k, o).wait()

        @pl.when(me < n - 1)
        def _():
            for owner in range(n):
                edge_copy(k, owner).wait_send()

        for e in mates:
            scatter_copy(k, e, dp).wait_send()
            gather_copy(k, e, dp).wait_send()
            share_copy(k, e, dp).wait_send()

    if fused:

        @pl.loop(0, chunks)
        def _(k):
            cols = columns(0, k)
            for e in mates:
                gather_copy(k, e, mate(e)).wait_recv()
            taps_ref[:, cols] = gathered[:, cols].astype(F32) / groups
            total = gs_sum[:, cols].astype(F32)
            for e in mates:
                share_copy(k, e, mate(e)).wait_recv()
            for e in mates:
                total += gs_all[mate(e), :, cols].astype(F32)
            write_shorts(cols, total / groups)

    for d in order:
        weight_copy(d, me).wait_send()

    @pl.when(me > 0)
    def _():
        to_earlier.wait_send()


def local(projected, token_ids, short_filters, medium_filter, skip_gain):
    inputs = projected[:, 0]
    _, block, channels = inputs.shape
    short_len = short_filters.shape[1]
    own = medium_filter.shape[1]
    groups = lax.axis_size("dp")
    n = lax.axis_size("ctx")
    chunks = max(1, own // 512)
    width = own // chunks
    table = transform_table(block)
    forward = jnp.asarray(table.astype(ml_dtypes.bfloat16))
    inverse = jnp.asarray((table.T / block).astype(ml_dtypes.bfloat16))
    rows = block + EDGE
    vmem = pl.BlockSpec(memory_space=pltpu.VMEM)
    hbm = pl.BlockSpec(memory_space=pl.ANY)
    dma = pltpu.SemaphoreType.DMA
    fused = block == EDGE * groups
    held = groups if fused else 1
    out, taps, short, gain = pl.pallas_call(
        functools.partial(kernel, n, groups, chunks, fused),
        out_shape=(
            jax.ShapeDtypeStruct(inputs.shape, BF16),
            jax.ShapeDtypeStruct((block, own), F32),
            jax.ShapeDtypeStruct((short_len, 2, own), F32),
            jax.ShapeDtypeStruct((1, own), F32),
        ),
        in_specs=[hbm] * 7,
        out_specs=(hbm, vmem, vmem, vmem),
        scratch_shapes=[
            pltpu.VMEM((1, block), jnp.int32),
            pltpu.VMEM((block, own), BF16),
            pltpu.VMEM((1, own), F32),
            pltpu.VMEM((2 * block, block), BF16),
            pltpu.VMEM((block, 2 * block), BF16),
            pltpu.VMEM((block, own), BF16),
            pltpu.VMEM((held, EDGE, own), BF16),
            pltpu.VMEM((EDGE, own), BF16),
            pltpu.VMEM((block, own), BF16),
            pltpu.VMEM((EDGE, own), BF16),
            pltpu.VMEM((held, EDGE, own), BF16),
            pltpu.VMEM((2, block + 2 * EDGE, channels), BF16),
            pltpu.VMEM((2, block + 2 * EDGE, channels), F32),
            pltpu.VMEM((2, rows, channels), F32),
            pltpu.VMEM((n, short_len, 2, own), F32),
            pltpu.VMEM((n, 8, block), F32),
            pltpu.VMEM((n * block, LANES), F32),
            pltpu.VMEM((block, channels), BF16),
            pltpu.VMEM((n * block, own), BF16),
            pltpu.VMEM((n * block + EDGE, own), BF16),
            pltpu.VMEM((rows, channels), BF16),
            pltpu.VMEM((2, block, channels), BF16),
            pltpu.VMEM((2, rows, LANES), F32),
            pltpu.VMEM((EDGE, channels), F32),
            pltpu.VMEM((EDGE, channels), BF16),
            pltpu.VMEM((n, EDGE, own), BF16),
            pltpu.VMEM((n, 2 * block, width), F32),
            pltpu.VMEM((n, 2 * block, width), F32),
            pltpu.VMEM((n * block, width), BF16),
            dma((chunks, n)),
            dma((chunks, n)),
            dma,
            dma,
            dma((n,)),
            dma((n,)),
            dma((chunks, n)),
            dma((chunks, n)),
            dma((chunks, n)),
            dma((chunks, n)),
            dma((chunks, n)),
            dma((chunks, n)),
            dma((chunks, n)),
            dma((chunks, n)),
            dma((chunks, held)),
            dma((chunks, held)),
            dma((chunks, held)),
            dma((chunks, held)),
            dma((chunks, held)),
            dma((chunks, held)),
            dma((7,)),
            dma((chunks, n)),
        ],
        compiler_params=pltpu.CompilerParams(
            collective_id=0, has_side_effects=True, vmem_limit_bytes=60 * 1024 * 1024
        ),
    )(inputs, token_ids, short_filters.transpose(1, 0, 2), medium_filter, skip_gain[None], forward, inverse)
    if not fused:
        taps, short, gain = (
            lax.psum(part.astype(BF16), "dp").astype(F32) / groups for part in (taps, short, gain)
        )
    return out[:, None], short.transpose(1, 0, 2), taps, gain[0]


def solution(mesh):
    placed = (
        P(None, "dp", "ctx", None),
        P("dp", "ctx"),
        P(None, None, "ctx"),
        P(None, "ctx"),
        P("ctx"),
    )
    return jax.shard_map(
        local,
        mesh=mesh,
        in_specs=placed,
        out_specs=(P(None, "dp", "ctx", None), P(None, None, "ctx"), P(None, "ctx"), P("ctx")),
        check_vma=False,
    )
```
